32 devices in a mesh: row: 8 (over z, core), col: 4 (over y, x).
Axes of the slice: x: 2, y: 2, z: 4, core: 2. Of those that a mesh axis runs over, the one named last changes fastest.
Arguments:
- features: bfloat16 [4, 1024, 256], P('col', 'row'), may hold values from -6 to 6
- tiles: bfloat16 [8, 4, 3, 128, 128], P('row', 'col'), may hold values from -4 to 4
- tile_rows: int32 [8, 4, 3], P('row', 'col'), may hold values from 0 to 3, as said below
- tile_cols: int32 [8, 4, 3], P('row', 'col'), may hold values from 0 to 7, as said below
- tile_count: int32 [8, 4], P('row', 'col'), may hold values from 1 to 3, as said below
- weight: bfloat16 [256, 256], replicated, may hold values from -0.375 to 0.375
- bias: float32 [256], replicated, may hold values from -3 to 3
- cotangent: bfloat16 [8, 512, 256], P('row', 'col'), may hold values from -6 to 6
- label_mask: int32 [8, 512], P('row', 'col'), may hold values 0 or 1
Outputs:
- hidden: bfloat16 [8, 512, 256], P('row', 'col')
- grad_weight: float32 [256, 256], replicated
- grad_bias: float32 [256], replicated
- grad_features: bfloat16 [4, 1024, 256], P('col', 'row')
The draws below stay inside these ranges and needn't reach their ends.
Inputs may be any that keep to these rules, and one draw needn't show every extreme that they name: `tile_rows`: tile row among the 4 tile rows of a block; the (row, column) positions of one block's slots are all distinct. `tile_cols`: tile column among the 8 tile columns of a block. The live slots of a block are its first tile_count slots; some block has all 3 slots live.
All inputs are finite; a program needn't handle non-finite values. No bound on the sum of `label_mask` on one device may be relied on, other than what follows from the above.
Results may differ from the reference program's by a relative error of at most 0.023.
Values may be sent and summed in bfloat16 or wider, within the bound.
No kernel may reach another device: no remote copies, remote signals or barrier semaphores. Data moves between devices by JAX's collectives and lax.ppermute only.
A program may use at most 64 MiB of HBM per device.

```python
import math
import jax
import jax.numpy as jnp
from jax import lax

F = 256
TB = 128
RT = 1
R = 128
TMAX = 3
NODES = 4096
N_ROW = 8
N_COL = 4


def slot_positions(key):
    pattern_key = jax.random.fold_in(key, 11)
    positions = N_COL * RT * N_ROW * RT
    keys = jax.random.split(pattern_key, N_ROW * N_COL)
    picked = jax.vmap(lambda one_key: jax.random.permutation(one_key, positions)[:TMAX])(keys)
    return picked.reshape(N_ROW, N_COL, TMAX).astype(jnp.int32)


def draw_tile_rows(key, part):
    return slot_positions(key) // (N_ROW * RT)


def draw_tile_cols(key, part):
    return slot_positions(key) % (N_ROW * RT)


def draw_tile_count(key, part):
    count_key = jax.random.fold_in(key, 23)
    first_key, second_key, place_key = jax.random.split(count_key, 3)
    lowest = max(TMAX // 14, 1)
    spread_range = max(TMAX - lowest, 1)
    first = jax.random.randint(first_key, (N_ROW * N_COL,), 0, spread_range + 1)
    second = jax.random.randint(second_key, (N_ROW * N_COL,), 0, spread_range + 1)
    counts = jnp.minimum(lowest + first * second // spread_range, TMAX)
    place = jax.random.randint(place_key, (), 0, N_ROW * N_COL)
    counts = counts.at[place].set(TMAX)
    return counts.reshape(N_ROW, N_COL).astype(jnp.int32)


def with_ends(drawn, stream_key, least, top_value):
    spot = [jax.random.randint(jax.random.fold_in(stream_key, axis), (), 0, length) for axis, length in enumerate(drawn.shape)]
    longest = drawn.shape.index(max(drawn.shape))
    beside = spot[:longest] + [(spot[longest] + 1) % drawn.shape[longest]] + spot[longest + 1:]
    return drawn.at[tuple(spot)].set(least).at[tuple(beside)].set(top_value)


def block_scale(rng, extent, shards, least, largest):
    def one(dim, shards_of):
        heights = jax.random.uniform(jax.random.fold_in(jax.random.fold_in(rng, 6), dim), (shards_of,), jnp.float32, least / len(shards), largest / len(shards))
        return jnp.repeat(jnp.exp(heights), extent[dim] // shards_of).reshape((-1,) + (1,) * (len(extent) - dim - 1))

    factor_of = one(*shards[0])
    for cut in shards[1:]:
        factor_of = factor_of * one(*cut)
    return factor_of


def noise(rng, extent, width, reach, cuts=(), kind=jnp.bfloat16):
    array = width * jax.random.normal(rng, extent, jnp.float32)
    if cuts:
        array = array * block_scale(rng, extent, cuts, -0.22, 0.18)
    return jnp.clip(array, -reach, reach).astype(kind)


def setup_inputs(seed: int = 0) -> dict:
    key_of = jax.random.split(jax.random.key(seed), 10)
    return {
        "features": noise(key_of[0], (N_COL, N_ROW * R, F), 1.0, 6.0, ((0, 4), (1, 8))),
        "tiles": noise(key_of[1], (N_ROW, N_COL, TMAX, TB, TB), ((TMAX * N_COL) ** -0.5), 4.0, ((0, 8), (1, 4))),
        "tile_rows": draw_tile_rows(jax.random.fold_in(key_of[9], 71), 0),
        "tile_cols": draw_tile_cols(jax.random.fold_in(key_of[9], 71), 0),
        "tile_count": draw_tile_count(jax.random.fold_in(key_of[9], 71), 0),
        "weight": noise(key_of[5], (F, F), F ** -0.5, 0.375),
        "bias": noise(key_of[6], (F,), 0.5, 3.0, (), jnp.float32),
        "cotangent": noise(key_of[7], (N_ROW, N_COL * R, F), 1.0, 6.0, ((0, 8), (1, 4))),
        "label_mask": with_ends((jax.random.randint(key_of[8], (N_ROW, N_COL * R), 0, 3) < 1).astype(jnp.int32), jax.random.fold_in(key_of[8], 1), 0, 1),
    }


def spread(block_tiles, take_index, put_index, live_count, source, out_tiles, transpose):
    picked = source[take_index].astype(jnp.float32)
    block = block_tiles.astype(jnp.float32)
    if transpose:
        product = jnp.einsum('sij,sif->sjf', block, picked)
    else:
        product = jnp.einsum('sij,sjf->sif', block, picked)
    live = jnp.arange(block_tiles.shape[0], dtype=jnp.int32) < live_count
    product = jnp.where(live[:, None, None], product, jnp.float32(0.0))
    empty = jnp.zeros((out_tiles, TB, F), jnp.float32)
    return empty.at[put_index].add(product)

def reference(features, tiles, tile_rows, tile_cols, tile_count, weight, bias, cotangent, label_mask):
    col_tiles = N_ROW * R // TB
    row_tiles = N_COL * R // TB

    def forward_row(r_index):

        def step(total, c_index):
            source = features[c_index].reshape(col_tiles, TB, F)
            term = spread(tiles[r_index, c_index], tile_cols[r_index, c_index], tile_rows[r_index, c_index], tile_count[r_index, c_index], source, row_tiles, False)
            return (total + term, None)
        total, _ = lax.scan(step, jnp.zeros((row_tiles, TB, F), jnp.float32), jnp.arange(N_COL, dtype=jnp.int32))
        return total.reshape(N_COL * R, F)
    aggregated = lax.map(forward_row, jnp.arange(N_ROW, dtype=jnp.int32)).astype(jnp.bfloat16)
    flat = aggregated.reshape(NODES, F)
    pre_act = jnp.dot(flat, weight, preferred_element_type=jnp.float32) + bias
    sigma = jax.nn.sigmoid(pre_act)
    hidden = (pre_act * sigma).astype(jnp.bfloat16).reshape(N_ROW, N_COL * R, F)
    kept = label_mask.reshape(NODES).astype(jnp.float32)[:, None]
    slope = sigma * (1.0 + pre_act * (1.0 - sigma))
    grad_pre = (cotangent.reshape(NODES, F).astype(jnp.float32) * kept * slope).astype(jnp.bfloat16)
    scale = 1.0 / math.sqrt(NODES)
    grad_weight = jnp.dot(flat.T, grad_pre, preferred_element_type=jnp.float32) * scale
    grad_bias = lax.optimization_barrier(jnp.sum(grad_pre.astype(jnp.float32), axis=0)) * scale
    grad_agg = jnp.dot(grad_pre, weight.T, preferred_element_type=jnp.float32).astype(jnp.bfloat16).reshape(N_ROW, N_COL * R, F)

    def backward_col(c_index):

        def step(total, r_index):
            source = grad_agg[r_index].reshape(row_tiles, TB, F)
            term = spread(tiles[r_index, c_index], tile_rows[r_index, c_index], tile_cols[r_index, c_index], tile_count[r_index, c_index], source, col_tiles, True)
            term = lax.optimization_barrier(term.astype(jnp.bfloat16)).astype(jnp.float32)
            return (total + term, None)
        total, _ = lax.scan(step, jnp.zeros((col_tiles, TB, F), jnp.float32), jnp.arange(N_ROW, dtype=jnp.int32))
        return total.reshape(N_ROW * R, F)
    grad_features = lax.map(backward_col, jnp.arange(N_COL, dtype=jnp.int32)).astype(jnp.bfloat16)
    return (hidden, grad_weight, grad_bias, grad_features)
```

```python
import functools
import math

import jax
import jax.numpy as jnp
from jax import lax
from jax.experimental import pallas as pl
from jax.experimental.pallas import tpu as pltpu
from jax.sharding import PartitionSpec as P

F32 = jnp.float32
BF16 = jnp.bfloat16
PAD = 16
ROWS_ROWS = (((0,), (0,)), ((), ()))
COLS_COLS = (((1,), (1,)), ((), ()))


def each(count, body):
    if count <= 16:
        for i in range(count):
            body(i)
    else:
        lax.fori_loop(0, count, lambda i, carry: (body(i), carry)[1], 0)


def exchange(value, axis, mask):
    size = lax.axis_size(axis)
    return lax.ppermute(value, axis, [(i, i ^ mask) for i in range(size)])


def tree_sum(terms):
    terms = list(terms)
    while len(terms) > 1:
        terms = [a + b for a, b in zip(terms[::2], terms[1::2], strict=True)]
    return terms[0]


def two_halves(row):
    high = row.astype(BF16)
    low = (row - high.astype(F32)).astype(BF16)
    place = lax.broadcasted_iota(jnp.int32, (PAD, row.shape[-1]), 0)
    block = jnp.where(place == 0, high.astype(F32), jnp.where(place == 1, low.astype(F32), 0.0))
    return block.astype(BF16)


def joined(block):
    rows = block.astype(F32)
    return rows[0:1] + rows[1:2]


def forward_kernel(slots, n_col, blocks, ints, tiles, *refs):
    n_row = len(refs) - 3
    sources, out, held, total = refs[:n_row], refs[n_row], refs[n_row + 1], refs[n_row + 2]
    side = tiles.shape[-1]
    for q in range(n_row):
        held[q] = sources[q][...]
    me_row, live = ints[0], ints[2]

    def product(s):
        taken = held[ints[3 + slots + s] ^ me_row]
        value = jnp.dot(tiles[s], taken, preferred_element_type=F32)
        return jnp.where(s < live, value, 0.0)

    if blocks == slots:
        for s in range(slots):
            out[s * side : (s + 1) * side] = product(s).astype(BF16)
        return
    total[...] = jnp.zeros_like(total)

    def add(s):
        total[ints[3 + s]] += product(s)

    each(slots, add)
    for t in range(n_col):
        out[t * side : (t + 1) * side] = total[t].astype(BF16)


def middle_kernel(slots, n_row, n_col, blocks, ints, weight, bias, tiles, *refs):
    products, refs = refs[:n_col], refs[n_col:]
    cots, refs = refs[:n_col], refs[n_col:]
    hidden, sent, kept, kept_weight, prods, total, agg, grads, grad_agg, weights, back = refs
    side = tiles.shape[-1]
    half = weight.shape[0] // 2
    me_row, me_col, live = ints[0], ints[1], ints[2]
    for q in range(n_col):
        prods[q] = products[q][...]
    total[...] = jnp.zeros_like(total)

    def add(i):
        c, p = i // blocks, i % blocks
        q = me_col ^ c
        start = p * side
        place = ints[3 + 2 * slots + q * blocks + p]
        total[place] += prods[q, pl.ds(start, side), :].astype(F32)

    each(n_col * blocks, add)
    for q in range(n_col):
        t = me_col ^ q
        rows = pl.ds(pl.multiple_of(t * side, side), side)
        aggregated = total[t].astype(BF16)
        agg[rows, :] = aggregated
        pre_act = jnp.dot(aggregated, weight[...], preferred_element_type=F32) + bias[...]
        sigma = jax.nn.sigmoid(pre_act)
        if q == 0:
            hidden[...] = (pre_act * sigma).astype(BF16)
        slope = sigma * (1.0 + pre_act * (1.0 - sigma))
        grad_pre = (cots[q][0:side].astype(F32) * slope).astype(BF16)
        grads[rows, :] = grad_pre
        grad_agg[t] = lax.dot_general(
            grad_pre, weight[...], COLS_COLS, preferred_element_type=F32
        ).astype(BF16)
    back[...] = jnp.zeros_like(back)

    def put(s):
        value = lax.dot_general(
            tiles[s], grad_agg[ints[3 + s]], ROWS_ROWS, preferred_element_type=F32
        )
        back[ints[3 + slots + s] ^ me_row] += jnp.where(s < live, value, 0.0)

    each(slots, put)
    for m in range(n_row // 2):
        kept[m * side : (m + 1) * side] = back[2 * m]
        sent[m * side : (m + 1) * side] = back[2 * m + 1].astype(BF16)
    weights[...] = lax.dot_general(
        agg[...], grads[...], ROWS_ROWS, preferred_element_type=F32
    ).reshape(weights.shape)
    core = me_row % 2
    after = n_row // 2 * side
    kept_weight[...] = weights[core]
    sent[after : after + half] = weights[1 - core].astype(BF16)
    column_sum = jnp.sum(grads[...].astype(F32), axis=0, keepdims=True)
    sent[after + half : after + half + PAD] = two_halves(column_sum)


def chip_kernel(kept, kept_weight, own_sent, came, mine, *outs):
    half, side = kept_weight.shape[0], mine.shape[0]
    after = kept.shape[0]
    mine[...] = kept[0:side] + came[0:side].astype(F32)
    weights = (kept_weight[...] + came[after : after + half].astype(F32)).astype(BF16)
    ends = slice(after + half, after + half + PAD)
    column_sum = two_halves(joined(own_sent[ends]) + joined(came[ends]))
    for m, out in enumerate(outs, 1):
        part = slice(m * side, (m + 1) * side)
        out[0:side] = (kept[part] + came[part].astype(F32)).astype(BF16)
        out[side : side + half] = weights
        out[side + half : side + half + PAD] = column_sum


def line_kernel(scale, mine, own, *refs):
    came, (grad_features, weights, grad_bias) = refs[:-3], refs[-3:]
    side, half = mine.shape[0], weights.shape[0]
    total = mine[...]
    for block in came:
        total = total + block[0:side].astype(F32)
    grad_features[...] = total.astype(BF16)
    everyone = (own, *came)
    weights[...] = scale * tree_sum(b[side : side + half].astype(F32) for b in everyone)
    grad_bias[...] = scale * tree_sum(joined(b[side + half : side + half + PAD]) for b in everyone)


def call(kernel, name, outs, scratch, ints, *arrays):
    specs = [pl.BlockSpec(memory_space=pltpu.VMEM)] * len(arrays)
    if ints is not None:
        specs = [pl.BlockSpec(memory_space=pltpu.SMEM)] + specs
        arrays = (ints, *arrays)
    return pl.pallas_call(
        kernel,
        name=name,
        out_shape=[jax.ShapeDtypeStruct(shape, dtype) for shape, dtype in outs],
        in_specs=specs,
        out_specs=[pl.BlockSpec(memory_space=pltpu.VMEM)] * len(outs),
        scratch_shapes=[pltpu.VMEM(shape, dtype) for shape, dtype in scratch],
        compiler_params=pltpu.CompilerParams(vmem_limit_bytes=56 * 1024 * 1024),
    )(*arrays)


def on_device(
    features, tiles, tile_rows, tile_cols, tile_count, weight, bias, cotangent, label_mask
):
    side = tiles.shape[-1]
    slots = tiles.shape[2]
    width = features.shape[2]
    n_row = lax.axis_size("row")
    n_col = lax.axis_size("col")
    n_line = n_row // 2
    blocks = min(slots, n_col)
    own_tiles = tiles[0, 0]
    ints = jnp.concatenate(
        [
            lax.axis_index("row").astype(jnp.int32)[None],
            lax.axis_index("col").astype(jnp.int32)[None],
            tile_count[0],
            tile_rows[0, 0],
            tile_cols[0, 0],
        ]
    )

    own = features[0]
    along = [own] + [exchange(own, "row", 2 * m) for m in range(1, n_line)]
    sources = [part for block in along for part in (block, exchange(block, "row", 1))]

    kept = label_mask[0].astype(BF16)[:, None]
    if blocks == slots:
        places = tile_rows[0, 0]
    else:
        places = jnp.arange(blocks, dtype=jnp.int32)
    places = jnp.pad(places, (0, -blocks % PAD))[:, None].astype(BF16)
    with_places = jnp.concatenate([cotangent[0] * kept, jnp.broadcast_to(places, (places.shape[0], width))])
    cots = [with_places] + [exchange(with_places, "col", m) for m in range(1, n_col)]

    (product,) = call(
        functools.partial(forward_kernel, slots, n_col, blocks),
        "tile_products",
        [((blocks * side, width), BF16)],
        [((n_row, side, width), BF16), ((n_col, side, width), F32)],
        ints,
        own_tiles,
        *sources,
    )
    products = [product] + [exchange(product, "col", m) for m in range(1, n_col)]
    all_ints = jnp.concatenate([ints] + [c[side : side + blocks, 0].astype(jnp.int32) for c in cots])
    after = n_line * side
    half = width // 2
    hidden, sent, kept_back, kept_weight = call(
        functools.partial(middle_kernel, slots, n_row, n_col, blocks),
        "dense_layer",
        [
            ((side, width), BF16),
            ((after + half + PAD, width), BF16),
            ((after, width), F32),
            ((half, width), F32),
        ],
        [
            ((n_col, blocks * side, width), BF16),
            ((n_col, side, width), F32),
            ((n_col * side, width), BF16),
            ((n_col * side, width), BF16),
            ((n_col, side, width), BF16),
            ((2, half, width), F32),
            ((n_row, side, width), F32),
        ],
        all_ints,
        weight,
        bias[None],
        own_tiles,
        *products,
        *cots,
    )
    came = exchange(sent, "row", 1)
    mine, *parts = call(
        chip_kernel,
        "chip_sums",
        [((side, width), F32)] + [((side + half + PAD, width), BF16)] * (n_line - 1),
        [],
        None,
        kept_back,
        kept_weight,
        sent,
        came,
    )
    came = [exchange(part, "row", 2 * m) for m, part in enumerate(parts, 1)]
    scale = 1.0 / math.sqrt(n_row * n_col * side)
    grad_features, weights, grad_bias = call(
        functools.partial(line_kernel, scale),
        "line_sums",
        [((side, width), BF16), ((half, width), F32), ((1, width), F32)],
        [],
        None,
        mine,
        parts[0],
        *came,
    )
    other = exchange(weights, "row", 1)
    first = lax.axis_index("row") % 2 == 0
    grad_weight = jnp.concatenate([jnp.where(first, weights, other), jnp.where(first, other, weights)])
    return (hidden[None], grad_weight, grad_bias[0], grad_features[None])


def solution(mesh):
    return jax.shard_map(
        on_device,
        mesh=mesh,
        in_specs=(
            P("col", "row", None),
            P("row", "col", None, None, None),
            P("row", "col", None),
            P("row", "col", None),
            P("row", "col"),
            P(),
            P(),
            P("row", "col", None),
            P("row", "col"),
        ),
        out_specs=(P("row", "col", None), P(), P(), P("col", "row", None)),
        check_vma=False,
    )
```

```python
import functools
import math

import jax
import jax.numpy as jnp
from jax import lax
from jax.experimental import pallas as pl
from jax.experimental.pallas import tpu as pltpu
from jax.sharding import PartitionSpec as P

F32 = jnp.float32
BF16 = jnp.bfloat16
PAD = 16
ROWS_ROWS = (((0,), (0,)), ((), ()))
COLS_COLS = (((1,), (1,)), ((), ()))


def each(count, body):
    if count <= 16:
        for i in range(count):
            body(i)
    else:
        lax.fori_loop(0, count, lambda i, carry: (body(i), carry)[1], 0)


def exchange(value, axis, mask):
    size = lax.axis_size(axis)
    return lax.ppermute(value, axis, [(i, i ^ mask) for i in range(size)])


def tree_sum(terms):
    terms = list(terms)
    while len(terms) > 1:
        terms = [a + b for a, b in zip(terms[::2], terms[1::2], strict=True)]
    return terms[0]


def two_halves(row):
    high = row.astype(BF16)
    low = (row - high.astype(F32)).astype(BF16)
    place = lax.broadcasted_iota(jnp.int32, (PAD, row.shape[-1]), 0)
    block = jnp.where(place == 0, high.astype(F32), jnp.where(place == 1, low.astype(F32), 0.0))
    return block.astype(BF16)


def joined(block):
    rows = block.astype(F32)
    return rows[0:1] + rows[1:2]


def cotangent_kernel(ints, mask, cotangent, out):
    side, width = cotangent.shape
    shape = (side, side)
    diagonal = lax.broadcasted_iota(jnp.int32, shape, 0) == lax.broadcasted_iota(jnp.int32, shape, 1)
    spread = jnp.where(diagonal, mask[...].astype(F32), 0.0).astype(BF16)
    out[0:side] = jnp.dot(spread, cotangent[...], preferred_element_type=F32).astype(BF16)
    rows = out.shape[0] - side
    index = lax.broadcasted_iota(jnp.int32, (rows, width), 0)
    places = jnp.zeros((rows, width), jnp.int32)
    for p in range(ints.shape[0]):
        places = jnp.where(index == p, ints[p], places)
    out[side:] = places.astype(F32).astype(BF16)


def forward_kernel(slots, n_col, blocks, ints, tiles, *refs):
    n_row = len(refs) - 3
    sources, out, held, total = refs[:n_row], refs[n_row], refs[n_row + 1], refs[n_row + 2]
    side = tiles.shape[-1]
    for q in range(n_row):
        held[q] = sources[q][...]
    me_row, live = ints[0], ints[2]

    def product(s):
        taken = held[ints[3 + slots + s] ^ me_row]
        value = jnp.dot(tiles[s], taken, preferred_element_type=F32)
        return jnp.where(s < live, value, 0.0)

    if blocks == slots:
        for s in range(slots):
            out[s * side : (s + 1) * side] = product(s).astype(BF16)
        return
    total[...] = jnp.zeros_like(total)

    def add(s):
        total[ints[3 + s]] += product(s)

    each(slots, add)
    for t in range(n_col):
        out[t * side : (t + 1) * side] = total[t].astype(BF16)


def middle_kernel(slots, n_row, n_col, blocks, ints, weight, bias, tiles, *refs):
    products, refs = refs[:n_col], refs[n_col:]
    cots, refs = refs[:n_col], refs[n_col:]
    hidden, sent, kept, kept_weight, prods, total, agg, grads, grad_agg, weights, back = refs
    side = tiles.shape[-1]
    half = weight.shape[0] // 2
    me_row, me_col, live = ints[0], ints[1], ints[2]
    for q in range(n_col):
        prods[q] = products[q][...]
    total[...] = jnp.zeros_like(total)

    def add(i):
        c, p = i // blocks, i % blocks
        q = me_col ^ c
        start = p * side
        place = ints[3 + 2 * slots + q * blocks + p]
        total[place] += prods[q, pl.ds(start, side), :].astype(F32)

    each(n_col * blocks, add)
    for q in range(n_col):
        t = me_col ^ q
        rows = pl.ds(pl.multiple_of(t * side, side), side)
        aggregated = total[t].astype(BF16)
        agg[rows, :] = aggregated
        pre_act = jnp.dot(aggregated, weight[...], preferred_element_type=F32) + bias[...]
        sigma = jax.nn.sigmoid(pre_act)
        if q == 0:
            hidden[...] = (pre_act * sigma).astype(BF16)
        slope = sigma * (1.0 + pre_act * (1.0 - sigma))
        grad_pre = (cots[q][0:side].astype(F32) * slope).astype(BF16)
        grads[rows, :] = grad_pre
        grad_agg[t] = lax.dot_general(
            grad_pre, weight[...], COLS_COLS, preferred_element_type=F32
        ).astype(BF16)
    back[...] = jnp.zeros_like(back)

    def put(s):
        value = lax.dot_general(
            tiles[s], grad_agg[ints[3 + s]], ROWS_ROWS, preferred_element_type=F32
        )
        back[ints[3 + slots + s] ^ me_row] += jnp.where(s < live, value, 0.0)

    each(slots, put)
    for m in range(n_row // 2):
        kept[m * side : (m + 1) * side] = back[2 * m]
        sent[m * side : (m + 1) * side] = back[2 * m + 1].astype(BF16)
    weights[...] = lax.dot_general(
        agg[...], grads[...], ROWS_ROWS, preferred_element_type=F32
    ).reshape(weights.shape)
    core = me_row % 2
    after = n_row // 2 * side
    kept_weight[...] = weights[core]
    sent[after : after + half] = weights[1 - core].astype(BF16)
    column_sum = jnp.sum(grads[...].astype(F32), axis=0, keepdims=True)
    sent[after + half : after + half + PAD] = two_halves(column_sum)


def chip_kernel(kept, kept_weight, own_sent, came, mine, *outs):
    half, side = kept_weight.shape[0], mine.shape[0]
    after = kept.shape[0]
    mine[...] = kept[0:side] + came[0:side].astype(F32)
    weights = (kept_weight[...] + came[after : after + half].astype(F32)).astype(BF16)
    ends = slice(after + half, after + half + PAD)
    column_sum = two_halves(joined(own_sent[ends]) + joined(came[ends]))
    for m, out in enumerate(outs, 1):
        part = slice(m * side, (m + 1) * side)
        out[0:side] = (kept[part] + came[part].astype(F32)).astype(BF16)
        out[side : side + half] = weights
        out[side + half : side + half + PAD] = column_sum


def line_kernel(scale, core, mine, *refs):
    blocks, (grad_features, grad_weight, grad_bias) = refs[:-3], refs[-3:]
    side, half = mine.shape[0], grad_weight.shape[0] // 2
    own, other = blocks[: len(blocks) // 2], blocks[len(blocks) // 2 :]
    total = mine[...]
    for block in own[1:]:
        total = total + block[0:side].astype(F32)
    grad_features[...] = total.astype(BF16)
    for shift, group in enumerate((own, other)):
        start = pl.multiple_of((core[0] ^ shift) * half, half)
        grad_weight[pl.ds(start, half), :] = scale * tree_sum(
            b[side : side + half].astype(F32) for b in group
        )
    grad_bias[...] = scale * tree_sum(joined(b[side + half : side + half + PAD]) for b in own)


def call(kernel, name, outs, scratch, ints, *arrays):
    arrays = [pltpu.with_memory_space_constraint(array, pltpu.VMEM) for array in arrays]
    specs = [pl.BlockSpec(memory_space=pltpu.VMEM)] * len(arrays)
    if ints is not None:
        specs = [pl.BlockSpec(memory_space=pltpu.SMEM)] + specs
        arrays = (ints, *arrays)
    need = sum(math.prod(shape) * jnp.dtype(dtype).itemsize for shape, dtype in scratch)
    return pl.pallas_call(
        kernel,
        name=name,
        out_shape=[
            pltpu.VMEM(shape, dtype) if stays else jax.ShapeDtypeStruct(shape, dtype)
            for shape, dtype, stays in outs
        ],
        in_specs=specs,
        out_specs=[pl.BlockSpec(memory_space=pltpu.VMEM)] * len(outs),
        scratch_shapes=[pltpu.VMEM(shape, dtype) for shape, dtype in scratch],
        compiler_params=pltpu.CompilerParams(vmem_limit_bytes=need + 8 * 1024 * 1024),
    )(*arrays)


def on_device(
    features, tiles, tile_rows, tile_cols, tile_count, weight, bias, cotangent, label_mask
):
    side = tiles.shape[-1]
    slots = tiles.shape[2]
    width = features.shape[2]
    n_row = lax.axis_size("row")
    n_col = lax.axis_size("col")
    n_line = n_row // 2
    blocks = min(slots, n_col)
    own_tiles = tiles[0, 0]
    me_row = lax.axis_index("row").astype(jnp.int32)[None]
    me_col = lax.axis_index("col").astype(jnp.int32)[None]
    ints = jnp.concatenate([me_row, me_col, tile_count[0], tile_rows[0, 0], tile_cols[0, 0]])

    own = features[0]
    along = [own] + [exchange(own, "row", 2 * m) for m in range(1, n_line)]
    sources = [part for block in along for part in (block, exchange(block, "row", 1))]

    if blocks == slots:
        places = tile_rows[0, 0]
    else:
        places = jnp.arange(blocks, dtype=jnp.int32)
    cotangent, _ = lax.optimization_barrier((cotangent[0], sources[1]))
    (with_places,) = call(
        cotangent_kernel,
        "masked_cotangent",
        [((side + blocks + -blocks % PAD, width), BF16, True)],
        [],
        places,
        label_mask,
        cotangent,
    )
    cots = [with_places] + [exchange(with_places, "col", m) for m in range(1, n_col)]

    (product,) = call(
        functools.partial(forward_kernel, slots, n_col, blocks),
        "tile_products",
        [((blocks * side, width), BF16, True)],
        [((n_row, side, width), BF16), ((n_col, side, width), F32)],
        ints,
        own_tiles,
        *sources,
    )
    products = [product] + [exchange(product, "col", m) for m in range(1, n_col)]
    all_ints = jnp.concatenate([ints] + [c[side : side + blocks, 0].astype(jnp.int32) for c in cots])
    after = n_line * side
    half = width // 2
    hidden, sent, kept_back, kept_weight = call(
        functools.partial(middle_kernel, slots, n_row, n_col, blocks),
        "dense_layer",
        [
            ((side, width), BF16, False),
            ((after + half + PAD, width), BF16, True),
            ((after, width), F32, True),
            ((half, width), F32, True),
        ],
        [
            ((n_col, blocks * side, width), BF16),
            ((n_col, side, width), F32),
            ((n_col * side, width), BF16),
            ((n_col * side, width), BF16),
            ((n_col, side, width), BF16),
            ((2, half, width), F32),
            ((n_row, side, width), F32),
        ],
        all_ints,
        weight,
        bias[None],
        own_tiles,
        *products,
        *cots,
    )
    came = exchange(sent, "row", 1)
    mine, *parts = call(
        chip_kernel,
        "chip_sums",
        [((side, width), F32, True)] + [((side + half + PAD, width), BF16, True)] * (n_line - 1),
        [],
        None,
        kept_back,
        kept_weight,
        sent,
        came,
    )
    line = [parts[0]] + [exchange(part, "row", 2 * m) for m, part in enumerate(parts, 1)]
    other = [exchange(block, "row", 1) for block in line]
    scale = 1.0 / math.sqrt(n_row * n_col * side)
    grad_features, grad_weight, grad_bias = call(
        functools.partial(line_kernel, scale),
        "line_sums",
        [((side, width), BF16, False), ((width, width), F32, False), ((1, width), F32, False)],
        [],
        me_row % 2,
        mine,
        *line,
        *other,
    )
    return (hidden[None], grad_weight, grad_bias[0], grad_features[None])


def solution(mesh):
    return jax.shard_map(
        on_device,
        mesh=mesh,
        in_specs=(
            P("col", "row", None),
            P("row", "col", None, None, None),
            P("row", "col", None),
            P("row", "col", None),
            P("row", "col"),
            P(),
            P(),
            P("row", "col", None),
            P("row", "col"),
        ),
        out_specs=(P("row", "col", None), P(), P(), P("col", "row", None)),
        check_vma=False,
    )
```

```python
import functools
import math

import jax
import jax.numpy as jnp
from jax import lax
from jax.experimental import pallas as pl
from jax.experimental.pallas import tpu as pltpu
from jax.sharding import PartitionSpec as P

F32 = jnp.float32
BF16 = jnp.bfloat16
PAD = 16
ROWS_ROWS = (((0,), (0,)), ((), ()))
COLS_COLS = (((1,), (1,)), ((), ()))


def each(count, body):
    if count <= 16:
        for i in range(count):
            body(i)
    else:
        lax.fori_loop(0, count, lambda i, carry: (body(i), carry)[1], 0)


def exchange(value, axis, mask):
    size = lax.axis_size(axis)
    return lax.ppermute(value, axis, [(i, i ^ mask) for i in range(size)])


def tree_sum(terms):
    terms = list(terms)
    while len(terms) > 1:
        terms = [a + b for a, b in zip(terms[::2], terms[1::2], strict=True)]
    return terms[0]


def two_halves(row):
    high = row.astype(BF16)
    low = (row - high.astype(F32)).astype(BF16)
    place = lax.broadcasted_iota(jnp.int32, (PAD, row.shape[-1]), 0)
    block = jnp.where(place == 0, high.astype(F32), jnp.where(place == 1, low.astype(F32), 0.0))
    return block.astype(BF16)


def joined(block):
    rows = block.astype(F32)
    return rows[0:1] + rows[1:2]


def cotangent_kernel(places, mask, cotangent, out):
    side, width = cotangent.shape
    shape = (side, side)
    diagonal = lax.broadcasted_iota(jnp.int32, shape, 0) == lax.broadcasted_iota(jnp.int32, shape, 1)
    spread = jnp.where(diagonal, mask[...].astype(F32), 0.0).astype(BF16)
    out[0:side] = jnp.dot(spread, cotangent[...], preferred_element_type=F32).astype(BF16)
    rows = out.shape[0] - side
    index = lax.broadcasted_iota(jnp.int32, (rows, width), 0)
    block = jnp.zeros((rows, width), jnp.int32)
    for p in range(places.shape[0]):
        block = jnp.where(index == p, places[p], block)
    out[side:] = block.astype(F32).astype(BF16)


def stack_kernel(*refs):
    out, start = refs[-1], 0
    for block in refs[:-1]:
        out[start : start + block.shape[0]] = block[...]
        start += block.shape[0]


def forward_kernel(slots, n_col, blocks, row, count, tile_rows, tile_cols, tiles, *refs):
    n_row = len(refs) - 3
    sources, out, held, total = refs[:n_row], refs[n_row], refs[n_row + 1], refs[n_row + 2]
    side = tiles.shape[-1]
    for q in range(n_row):
        held[q] = sources[q][...]
    me_row, live = row[0], count[0]

    def product(s):
        taken = held[tile_cols[s] ^ me_row]
        value = jnp.dot(tiles[s], taken, preferred_element_type=F32)
        return jnp.where(s < live, value, 0.0)

    if blocks == slots:
        for s in range(slots):
            out[s * side : (s + 1) * side] = product(s).astype(BF16)
        return
    total[...] = jnp.zeros_like(total)

    def add(s):
        total[tile_rows[s]] += product(s)

    each(slots, add)
    for t in range(n_col):
        out[t * side : (t + 1) * side] = total[t].astype(BF16)


def middle_kernel(slots, n_row, n_col, blocks, *refs):
    (row, col, count, tile_rows, tile_cols), refs = refs[:5], refs[5:]
    places, refs = refs[:n_col], refs[n_col:]
    (weight, bias, tiles, products), refs = refs[:4], refs[4:]
    steps = n_col.bit_length()
    cots, refs = refs[:steps], refs[steps:]
    hidden, sent, kept, kept_weight, total, agg, grads, grad_agg, weights, back, target = refs
    side = tiles.shape[-1]
    half = weight.shape[0] // 2
    me_row, me_col, live = row[0], col[0], count[0]
    total[...] = jnp.zeros_like(total)

    for q in range(n_col):
        for p in range(blocks):
            target[q, p] = places[q][p]

    def add(i):
        c, p = i // blocks, i % blocks
        q = me_col ^ c
        total[target[q, p]] += products[c, pl.ds(p * side, side), :].astype(F32)

    each(n_col * blocks, add)
    for q in range(n_col):
        t = me_col ^ q
        rows = pl.ds(pl.multiple_of(t * side, side), side)
        aggregated = total[t].astype(BF16)
        agg[rows, :] = aggregated
        pre_act = jnp.dot(aggregated, weight[...], preferred_element_type=F32) + bias[...]
        sigma = jax.nn.sigmoid(pre_act)
        if q == 0:
            hidden[...] = (pre_act * sigma).astype(BF16)
        slope = sigma * (1.0 + pre_act * (1.0 - sigma))
        step = q.bit_length()
        start = (q - (1 << step >> 1)) * cots[0].shape[0]
        cotangent = cots[step][start : start + side]
        grad_pre = (cotangent.astype(F32) * slope).astype(BF16)
        grads[rows, :] = grad_pre
        grad_agg[t] = lax.dot_general(
            grad_pre, weight[...], COLS_COLS, preferred_element_type=F32
        ).astype(BF16)
    back[...] = jnp.zeros_like(back)

    def put(s):
        value = lax.dot_general(
            tiles[s], grad_agg[tile_rows[s]], ROWS_ROWS, preferred_element_type=F32
        )
        back[tile_cols[s] ^ me_row] += jnp.where(s < live, value, 0.0)

    each(slots, put)
    for m in range(n_row // 2):
        kept[m * side : (m + 1) * side] = back[2 * m]
        sent[m * side : (m + 1) * side] = back[2 * m + 1].astype(BF16)
    weights[...] = lax.dot_general(
        agg[...], grads[...], ROWS_ROWS, preferred_element_type=F32
    ).reshape(weights.shape)
    core = me_row % 2
    after = n_row // 2 * side
    kept_weight[...] = weights[core]
    sent[after : after + half] = weights[1 - core].astype(BF16)
    column_sum = jnp.sum(grads[...].astype(F32), axis=0, keepdims=True)
    sent[after + half : after + half + PAD] = two_halves(column_sum)


def chip_kernel(kept, kept_weight, own_sent, came, mine, *outs):
    half, side = kept_weight.shape[0], mine.shape[0]
    after = kept.shape[0]
    mine[...] = kept[0:side] + came[0:side].astype(F32)
    weights = (kept_weight[...] + came[after : after + half].astype(F32)).astype(BF16)
    ends = slice(after + half, after + half + PAD)
    column_sum = two_halves(joined(own_sent[ends]) + joined(came[ends]))
    for m, out in enumerate(outs, 1):
        part = slice(m * side, (m + 1) * side)
        out[0:side] = (kept[part] + came[part].astype(F32)).astype(BF16)
        out[side : side + half] = weights
        out[side + half : side + half + PAD] = column_sum


def line_kernel(scale, row, mine, *refs):
    blocks, (grad_features, grad_weight, grad_bias) = refs[:-3], refs[-3:]
    side, half = mine.shape[0], grad_weight.shape[0] // 2
    own, other = blocks[: len(blocks) // 2], blocks[len(blocks) // 2 :]
    total = mine[...]
    for block in own[1:]:
        total = total + block[0:side].astype(F32)
    grad_features[...] = total.astype(BF16)
    for shift, group in enumerate((own, other)):
        start = pl.multiple_of((row[0] % 2 ^ shift) * half, half)
        grad_weight[pl.ds(start, half), :] = scale * tree_sum(
            b[side : side + half].astype(F32) for b in group
        )
    grad_bias[...] = scale * tree_sum(joined(b[side + half : side + half + PAD]) for b in own)


def call(kernel, name, outs, scratch, ints, *arrays):
    need = sum(math.prod(shape) * jnp.dtype(dtype).itemsize for shape, dtype in scratch)
    return pl.pallas_call(
        kernel,
        name=name,
        out_shape=[
            pltpu.VMEM(shape, dtype) if stays else jax.ShapeDtypeStruct(shape, dtype)
            for shape, dtype, stays in outs
        ],
        in_specs=[pl.BlockSpec(memory_space=pltpu.SMEM)] * len(ints)
        + [pl.BlockSpec(memory_space=pltpu.VMEM)] * len(arrays),
        out_specs=[pl.BlockSpec(memory_space=pltpu.VMEM)] * len(outs),
        scratch_shapes=[
            (pltpu.SMEM if dtype == jnp.int32 else pltpu.VMEM)(shape, dtype) for shape, dtype in scratch
        ],
        compiler_params=pltpu.CompilerParams(vmem_limit_bytes=need + 8 * 1024 * 1024),
    )(*ints, *arrays)


def near(array):
    return pltpu.with_memory_space_constraint(array, pltpu.VMEM)


def far(array):
    return pltpu.with_memory_space_constraint(array, pltpu.HBM)


def on_device(
    features, tiles, tile_rows, tile_cols, tile_count, weight, bias, cotangent, label_mask
):
    side = tiles.shape[-1]
    slots = tiles.shape[2]
    width = features.shape[2]
    n_row = lax.axis_size("row")
    n_col = lax.axis_size("col")
    n_line = n_row // 2
    blocks = min(slots, n_col)
    own_tiles = near(tiles[0, 0])
    row = lax.axis_index("row").astype(jnp.int32)[None]
    col = lax.axis_index("col").astype(jnp.int32)[None]
    ints = (tile_count[0], far(tile_rows[0, 0]), far(tile_cols[0, 0]))

    own = features[0]
    along = [own] + [exchange(own, "row", 2 * m) for m in range(1, n_line)]

    if blocks == slots:
        places = tile_rows[0, 0]
    else:
        places = jnp.arange(blocks, dtype=jnp.int32)
    (with_places,) = call(
        cotangent_kernel,
        "masked_cotangent",
        [((side + blocks + -blocks % PAD, width), BF16, True)],
        [],
        [far(places)],
        far(label_mask),
        far(cotangent[0]),
    )
    cots, reach = [with_places], 1
    while reach < n_col:
        (held,) = call(
            stack_kernel,
            "cotangents_so_far",
            [((reach * with_places.shape[0], width), BF16, True)],
            [],
            [],
            *map(near, cots),
        ) if reach > 1 else cots
        cots, reach = cots + [exchange(held, "col", reach)], 2 * reach

    along, cots[0] = lax.optimization_barrier((along, cots[0]))
    sources = [part for block in along for part in (block, exchange(block, "row", 1))]
    (product,) = call(
        functools.partial(forward_kernel, slots, n_col, blocks),
        "tile_products",
        [((blocks * side, width), BF16, True)],
        [((n_row, side, width), BF16), ((n_col, side, width), F32)],
        [row, *ints],
        own_tiles,
        *map(near, sources),
    )
    products = lax.all_gather(product, "col")
    each_rows = with_places.shape[0]
    everyones = [
        block[start + side : start + side + blocks, 0].astype(jnp.int32)
        for block in cots
        for start in range(0, block.shape[0], each_rows)
    ]
    after = n_line * side
    half = width // 2
    hidden, sent, kept_back, kept_weight = call(
        functools.partial(middle_kernel, slots, n_row, n_col, blocks),
        "dense_layer",
        [
            ((side, width), BF16, False),
            ((after + half + PAD, width), BF16, True),
            ((after, width), F32, True),
            ((half, width), F32, True),
        ],
        [
            ((n_col, side, width), F32),
            ((n_col * side, width), BF16),
            ((n_col * side, width), BF16),
            ((n_col, side, width), BF16),
            ((2, half, width), F32),
            ((n_row, side, width), F32),
            ((n_col, blocks), jnp.int32),
        ],
        [row, col, *ints, *everyones],
        near(weight),
        far(bias[None]),
        own_tiles,
        near(products),
        *map(near, cots),
    )
    came = exchange(sent, "row", 1)
    mine, *parts = call(
        chip_kernel,
        "chip_sums",
        [((side, width), F32, True)] + [((side + half + PAD, width), BF16, True)] * (n_line - 1),
        [],
        [],
        *map(near, (kept_back, kept_weight, sent, came)),
    )
    line = [parts[0]] + [exchange(part, "row", 2 * m) for m, part in enumerate(parts, 1)]
    other = [exchange(block, "row", 1) for block in line]
    scale = 1.0 / math.sqrt(n_row * n_col * side)
    grad_features, grad_weight, grad_bias = call(
        functools.partial(line_kernel, scale),
        "line_sums",
        [((side, width), BF16, False), ((width, width), F32, False), ((1, width), F32, False)],
        [],
        [row],
        *map(near, (mine, *line, *other)),
    )
    return (hidden[None], grad_weight, grad_bias[0], grad_features[None])


def solution(mesh):
    return jax.shard_map(
        on_device,
        mesh=mesh,
        in_specs=(
            P("col", "row", None),
            P("row", "col", None, None, None),
            P("row", "col", None),
            P("row", "col", None),
            P("row", "col"),
            P(),
            P(),
            P("row", "col", None),
            P("row", "col"),
        ),
        out_specs=(P("row", "col", None), P(), P(), P("col", "row", None)),
        check_vma=False,
    )
```

```python
import functools
import math

import jax
import jax.numpy as jnp
from jax import lax
from jax.experimental import pallas as pl
from jax.experimental.pallas import tpu as pltpu
from jax.sharding import PartitionSpec as P

F32 = jnp.float32
BF16 = jnp.bfloat16
PAD = 16
ROWS_ROWS = (((0,), (0,)), ((), ()))
COLS_COLS = (((1,), (1,)), ((), ()))


def each(count, body):
    if count <= 16:
        for i in range(count):
            body(i)
    else:
        lax.fori_loop(0, count, lambda i, carry: (body(i), carry)[1], 0)


def exchange(value, axis, mask):
    size = lax.axis_size(axis)
    return lax.ppermute(value, axis, [(i, i ^ mask) for i in range(size)])


def tree_sum(terms):
    terms = list(terms)
    while len(terms) > 1:
        terms = [a + b for a, b in zip(terms[::2], terms[1::2], strict=True)]
    return terms[0]


def two_halves(row):
    high = row.astype(BF16)
    low = (row - high.astype(F32)).astype(BF16)
    place = lax.broadcasted_iota(jnp.int32, (PAD, row.shape[-1]), 0)
    block = jnp.where(place == 0, high.astype(F32), jnp.where(place == 1, low.astype(F32), 0.0))
    return block.astype(BF16)


def joined(block):
    rows = block.astype(F32)
    return rows[0:1] + rows[1:2]


def cotangent_kernel(blocks, tile_rows, tile_cols, count, mask, cotangent, bias, out, own_bias, ints):
    own_bias[...] = bias[...]
    slots = tile_rows.shape[0]
    ints[2 * slots] = jnp.max(count[...])
    for s in range(slots):
        ints[s] = tile_rows[s]
        ints[slots + s] = tile_cols[s]
    side, width = cotangent.shape
    shape = (side, side)
    diagonal = lax.broadcasted_iota(jnp.int32, shape, 0) == lax.broadcasted_iota(jnp.int32, shape, 1)
    spread = jnp.where(diagonal, mask[...].astype(F32), 0.0).astype(BF16)
    out[0:side] = jnp.dot(spread, cotangent[...], preferred_element_type=F32).astype(BF16)
    rows = out.shape[0] - side
    index = lax.broadcasted_iota(jnp.int32, (rows, width), 0)
    block = jnp.zeros((rows, width), jnp.int32)
    for p in range(blocks):
        block = jnp.where(index == p, tile_rows[p] if blocks == slots else p, block)
    out[side:] = block.astype(F32).astype(BF16)


def stack_kernel(*refs):
    out, start = refs[-1], 0
    for block in refs[:-1]:
        out[start : start + block.shape[0]] = block[...]
        start += block.shape[0]


def forward_kernel(slots, n_col, blocks, ints, tiles, *refs):
    n_row = len(refs) - 3
    sources, out, held, total = refs[:n_row], refs[n_row], refs[n_row + 1], refs[n_row + 2]
    side = tiles.shape[-1]
    for q in range(n_row):
        held[q] = sources[q][...]
    me_row, live = lax.axis_index("row"), ints[2 * slots]

    def product(s):
        taken = held[ints[slots + s] ^ me_row]
        value = jnp.dot(tiles[s], taken, preferred_element_type=F32)
        return jnp.where(s < live, value, 0.0)

    if blocks == slots:
        for s in range(slots):
            out[s * side : (s + 1) * side] = product(s).astype(BF16)
        return
    total[...] = jnp.zeros_like(total)

    def add(s):
        total[ints[s]] += product(s)

    each(slots, add)
    for t in range(n_col):
        out[t * side : (t + 1) * side] = total[t].astype(BF16)


def middle_kernel(slots, n_row, n_col, blocks, *refs):
    ints, refs = refs[0], refs[1:]
    (weight, bias, tiles, products), refs = refs[:4], refs[4:]
    steps = n_col.bit_length()
    cots, refs = refs[:steps], refs[steps:]
    hidden, sent, kept, kept_weight, total, agg, grads, grad_agg, weights, back, target = refs
    side = tiles.shape[-1]
    half = weight.shape[0] // 2
    me_row, me_col, live = lax.axis_index("row"), lax.axis_index("col"), ints[2 * slots]
    each_rows = cots[0].shape[0]

    def cotangent(q, start, stop):
        step = q.bit_length()
        first = (q - (1 << step >> 1)) * each_rows
        return cots[step][first + start : first + stop]

    for q in range(n_col):
        places = cotangent(q, side, each_rows)[:, 0:128].astype(F32).astype(jnp.int32)
        for p in range(blocks):
            target[q, p] = jnp.max(places[p : p + 1])
    total[...] = jnp.zeros_like(total)

    def add(i):
        c, p = i // blocks, i % blocks
        q = me_col ^ c
        total[target[q, p]] += products[c, pl.ds(p * side, side), :].astype(F32)

    each(n_col * blocks, add)
    for q in range(n_col):
        t = me_col ^ q
        rows = pl.ds(pl.multiple_of(t * side, side), side)
        aggregated = total[t].astype(BF16)
        agg[rows, :] = aggregated
        pre_act = jnp.dot(aggregated, weight[...], preferred_element_type=F32) + bias[...]
        sigma = jax.nn.sigmoid(pre_act)
        if q == 0:
            hidden[...] = (pre_act * sigma).astype(BF16)
        slope = sigma * (1.0 + pre_act * (1.0 - sigma))
        grad_pre = (cotangent(q, 0, side).astype(F32) * slope).astype(BF16)
        grads[rows, :] = grad_pre
        grad_agg[t] = lax.dot_general(
            grad_pre, weight[...], COLS_COLS, preferred_element_type=F32
        ).astype(BF16)
    back[...] = jnp.zeros_like(back)

    def put(s):
        value = lax.dot_general(
            tiles[s], grad_agg[ints[s]], ROWS_ROWS, preferred_element_type=F32
        )
        back[ints[slots + s] ^ me_row] += jnp.where(s < live, value, 0.0)

    each(slots, put)
    for m in range(n_row // 2):
        kept[m * side : (m + 1) * side] = back[2 * m]
        sent[m * side : (m + 1) * side] = back[2 * m + 1].astype(BF16)
    weights[...] = lax.dot_general(
        agg[...], grads[...], ROWS_ROWS, preferred_element_type=F32
    ).reshape(weights.shape)
    core = me_row % 2
    after = n_row // 2 * side
    kept_weight[...] = weights[core]
    sent[after : after + half] = weights[1 - core].astype(BF16)
    column_sum = jnp.sum(grads[...].astype(F32), axis=0, keepdims=True)
    sent[after + half : after + half + PAD] = two_halves(column_sum)


def chip_kernel(kept, kept_weight, own_sent, came, mine, *outs):
    half, side = kept_weight.shape[0], mine.shape[0]
    after = kept.shape[0]
    mine[...] = kept[0:side] + came[0:side].astype(F32)
    weights = (kept_weight[...] + came[after : after + half].astype(F32)).astype(BF16)
    ends = slice(after + half, after + half + PAD)
    column_sum = two_halves(joined(own_sent[ends]) + joined(came[ends]))
    for m, out in enumerate(outs, 1):
        part = slice(m * side, (m + 1) * side)
        out[0:side] = (kept[part] + came[part].astype(F32)).astype(BF16)
        out[side : side + half] = weights
        out[side + half : side + half + PAD] = column_sum


def line_kernel(scale, own_hidden, mine, *refs):
    blocks, (hidden, grad_features, grad_weight, grad_bias) = refs[:-4], refs[-4:]
    hidden[...] = own_hidden[...]
    side, half = mine.shape[0], grad_weight.shape[0] // 2
    own, other = blocks[: len(blocks) // 2], blocks[len(blocks) // 2 :]
    total = mine[...]
    for block in own[1:]:
        total = total + block[0:side].astype(F32)
    grad_features[...] = total.astype(BF16)
    for shift, group in enumerate((own, other)):
        start = pl.multiple_of((lax.axis_index("row") % 2 ^ shift) * half, half)
        grad_weight[pl.ds(start, half), :] = scale * tree_sum(
            b[side : side + half].astype(F32) for b in group
        )
    grad_bias[...] = scale * tree_sum(joined(b[side + half : side + half + PAD]) for b in own)


def call(kernel, name, outs, scratch, ints, *arrays):
    need = sum(math.prod(shape) * jnp.dtype(dtype).itemsize for shape, dtype in scratch)

    def space(dtype):
        return pltpu.SMEM if dtype == jnp.int32 else pltpu.VMEM

    return pl.pallas_call(
        kernel,
        name=name,
        out_shape=[
            space(dtype)(shape, dtype) if stays else jax.ShapeDtypeStruct(shape, dtype)
            for shape, dtype, stays in outs
        ],
        in_specs=[pl.BlockSpec(memory_space=pltpu.SMEM)] * len(ints)
        + [pl.BlockSpec(memory_space=pltpu.VMEM)] * len(arrays),
        out_specs=[pl.BlockSpec(memory_space=space(dtype)) for _, dtype, _ in outs],
        scratch_shapes=[space(dtype)(shape, dtype) for shape, dtype in scratch],
        compiler_params=pltpu.CompilerParams(vmem_limit_bytes=need + 8 * 1024 * 1024),
    )(*ints, *arrays)


def near(array):
    return pltpu.with_memory_space_constraint(array, pltpu.VMEM)


def far(array):
    return pltpu.with_memory_space_constraint(array, pltpu.HBM)


def on_device(
    features, tiles, tile_rows, tile_cols, tile_count, weight, bias, cotangent, label_mask
):
    side = tiles.shape[-1]
    slots = tiles.shape[2]
    width = features.shape[2]
    n_row = lax.axis_size("row")
    n_col = lax.axis_size("col")
    n_line = n_row // 2
    blocks = min(slots, n_col)
    own_tiles = near(tiles[0, 0])

    own = features[0]
    along = [own] + [exchange(own, "row", 2 * m) for m in range(1, n_line)]

    with_places, own_bias, ints = call(
        functools.partial(cotangent_kernel, blocks),
        "masked_cotangent",
        [((side + blocks + -blocks % PAD, width), BF16, True), ((1, width), F32, True), ((2 * slots + 1,), jnp.int32, True)],
        [],
        [far(tile_rows[0, 0]), far(tile_cols[0, 0])],
        tile_count,
        far(label_mask),
        far(cotangent[0]),
        far(bias[None]),
    )
    ints = pltpu.with_memory_space_constraint(ints, pltpu.SMEM)
    cots, reach = [with_places], 1
    while reach < n_col:
        (held,) = call(
            stack_kernel,
            "cotangents_so_far",
            [((reach * with_places.shape[0], width), BF16, True)],
            [],
            [],
            *map(near, cots),
        ) if reach > 1 else cots
        cots, reach = cots + [exchange(held, "col", reach)], 2 * reach

    sources = [part for block in along for part in (block, exchange(block, "row", 1))]
    (product,) = call(
        functools.partial(forward_kernel, slots, n_col, blocks),
        "tile_products",
        [((blocks * side, width), BF16, True)],
        [((n_row, side, width), BF16), ((n_col, side, width), F32)],
        [ints],
        own_tiles,
        *map(near, sources),
    )
    products = lax.all_gather(product, "col")
    after = n_line * side
    half = width // 2
    hidden, sent, kept_back, kept_weight = call(
        functools.partial(middle_kernel, slots, n_row, n_col, blocks),
        "dense_layer",
        [
            ((side, width), BF16, True),
            ((after + half + PAD, width), BF16, True),
            ((after, width), F32, True),
            ((half, width), F32, True),
        ],
        [
            ((n_col, side, width), F32),
            ((n_col * side, width), BF16),
            ((n_col * side, width), BF16),
            ((n_col, side, width), BF16),
            ((2, half, width), F32),
            ((n_row, side, width), F32),
            ((n_col, blocks), jnp.int32),
        ],
        [ints],
        near(weight),
        near(own_bias),
        own_tiles,
        near(products),
        *map(near, cots),
    )
    came = exchange(sent, "row", 1)
    mine, *parts = call(
        chip_kernel,
        "chip_sums",
        [((side, width), F32, True)] + [((side + half + PAD, width), BF16, True)] * (n_line - 1),
        [],
        [],
        *map(near, (kept_back, kept_weight, sent, came)),
    )
    line = [parts[0]] + [exchange(part, "row", 2 * m) for m, part in enumerate(parts, 1)]
    other = [exchange(block, "row", 1) for block in line]
    scale = 1.0 / math.sqrt(n_row * n_col * side)
    hidden, grad_features, grad_weight, grad_bias = call(
        functools.partial(line_kernel, scale),
        "line_sums",
        [
            ((side, width), BF16, False),
            ((side, width), BF16, False),
            ((width, width), F32, False),
            ((1, width), F32, False),
        ],
        [],
        [],
        *map(near, (hidden, mine, *line, *other)),
    )
    return (hidden[None], grad_weight, grad_bias[0], grad_features[None])


def solution(mesh):
    return jax.shard_map(
        on_device,
        mesh=mesh,
        in_specs=(
            P("col", "row", None),
            P("row", "col", None, None, None),
            P("row", "col", None),
            P("row", "col", None),
            P("row", "col"),
            P(),
            P(),
            P("row", "col", None),
            P("row", "col"),
        ),
        out_specs=(P("row", "col", None), P(), P(), P("col", "row", None)),
        check_vma=False,
    )
```

```python
import functools
import math

import jax
import jax.numpy as jnp
from jax import lax
from jax.experimental import pallas as pl
from jax.experimental.pallas import tpu as pltpu
from jax.sharding import PartitionSpec as P

F32 = jnp.float32
BF16 = jnp.bfloat16
PAD = 16
ROWS_ROWS = (((0,), (0,)), ((), ()))
COLS_COLS = (((1,), (1,)), ((), ()))


def each(count, body):
    if count <= 16:
        for i in range(count):
            body(i)
    else:
        lax.fori_loop(0, count, lambda i, carry: (body(i), carry)[1], 0)


def exchange(value, axis, mask):
    size = lax.axis_size(axis)
    return lax.ppermute(value, axis, [(i, i ^ mask) for i in range(size)])


def tree_sum(terms):
    terms = list(terms)
    while len(terms) > 1:
        terms = [a + b for a, b in zip(terms[::2], terms[1::2], strict=True)]
    return terms[0]


def two_halves(row):
    high = row.astype(BF16)
    low = (row - high.astype(F32)).astype(BF16)
    place = lax.broadcasted_iota(jnp.int32, (PAD, row.shape[-1]), 0)
    block = jnp.where(place == 0, high.astype(F32), jnp.where(place == 1, low.astype(F32), 0.0))
    return block.astype(BF16)


def joined(block):
    rows = block.astype(F32)
    return rows[0:1] + rows[1:2]


def cotangent_kernel(blocks, tile_rows, tile_cols, mask, cotangent, bias, out, own_bias, ints):
    own_bias[...] = bias[...]
    slots = tile_rows.shape[0]
    for s in range(slots):
        ints[s] = tile_rows[s]
        ints[slots + s] = tile_cols[s]
    side, width = cotangent.shape
    shape = (side, side)
    diagonal = lax.broadcasted_iota(jnp.int32, shape, 0) == lax.broadcasted_iota(jnp.int32, shape, 1)
    spread = jnp.where(diagonal, mask[...].astype(F32), 0.0).astype(BF16)
    out[0:side] = jnp.dot(spread, cotangent[...], preferred_element_type=F32).astype(BF16)
    rows = out.shape[0] - side
    index = lax.broadcasted_iota(jnp.int32, (rows, width), 0)
    block = jnp.zeros((rows, width), jnp.int32)
    for p in range(blocks):
        block = jnp.where(index == p, tile_rows[p] if blocks == slots else p, block)
    out[side:] = block.astype(F32).astype(BF16)


def stack_kernel(*refs):
    out, start = refs[-1], 0
    for block in refs[:-1]:
        out[start : start + block.shape[0]] = block[...]
        start += block.shape[0]


def forward_kernel(slots, n_col, blocks, ints, counts, tiles, *refs):
    n_row = len(refs) - 4
    sources, (out, count, held, total) = refs[:n_row], refs[n_row:]
    count[0] = jnp.max(counts[...])
    side = tiles.shape[-1]
    for q in range(n_row):
        held[q] = sources[q][...]
    me_row, live = lax.axis_index("row"), count[0]

    def product(s):
        taken = held[ints[slots + s] ^ me_row]
        value = jnp.dot(tiles[s], taken, preferred_element_type=F32)
        return jnp.where(s < live, value, 0.0)

    if blocks == slots:
        for s in range(slots):
            out[s * side : (s + 1) * side] = product(s).astype(BF16)
        return
    total[...] = jnp.zeros_like(total)

    def add(s):
        total[ints[s]] += product(s)

    each(slots, add)
    for t in range(n_col):
        out[t * side : (t + 1) * side] = total[t].astype(BF16)


def middle_kernel(slots, n_row, n_col, blocks, *refs):
    (ints, count), refs = refs[:2], refs[2:]
    (weight, bias, tiles, products), refs = refs[:4], refs[4:]
    steps = n_col.bit_length()
    cots, refs = refs[:steps], refs[steps:]
    hidden, sent, kept, kept_weight, total, agg, grads, grad_agg, weights, back, target = refs
    side = tiles.shape[-1]
    half = weight.shape[0] // 2
    me_row, me_col, live = lax.axis_index("row"), lax.axis_index("col"), count[0]
    each_rows = cots[0].shape[0]

    def cotangent(q, start, stop):
        step = q.bit_length()
        first = (q - (1 << step >> 1)) * each_rows
        return cots[step][first + start : first + stop]

    for q in range(n_col):
        places = cotangent(q, side, each_rows)[:, 0:128].astype(F32).astype(jnp.int32)
        for p in range(blocks):
            target[q, p] = jnp.max(places[p : p + 1])
    total[...] = jnp.zeros_like(total)

    def add(i):
        c, p = i // blocks, i % blocks
        q = me_col ^ c
        total[target[q, p]] += products[c, pl.ds(p * side, side), :].astype(F32)

    each(n_col * blocks, add)
    for q in range(n_col):
        t = me_col ^ q
        rows = pl.ds(pl.multiple_of(t * side, side), side)
        aggregated = total[t].astype(BF16)
        agg[rows, :] = aggregated
        pre_act = jnp.dot(aggregated, weight[...], preferred_element_type=F32) + bias[...]
        sigma = jax.nn.sigmoid(pre_act)
        if q == 0:
            hidden[...] = (pre_act * sigma).astype(BF16)
        slope = sigma * (1.0 + pre_act * (1.0 - sigma))
        grad_pre = (cotangent(q, 0, side).astype(F32) * slope).astype(BF16)
        grads[rows, :] = grad_pre
        grad_agg[t] = lax.dot_general(
            grad_pre, weight[...], COLS_COLS, preferred_element_type=F32
        ).astype(BF16)
    back[...] = jnp.zeros_like(back)

    def put(s):
        value = lax.dot_general(
            tiles[s], grad_agg[ints[s]], ROWS_ROWS, preferred_element_type=F32
        )
        back[ints[slots + s] ^ me_row] += jnp.where(s < live, value, 0.0)

    each(slots, put)
    for m in range(n_row // 2):
        kept[m * side : (m + 1) * side] = back[2 * m]
        sent[m * side : (m + 1) * side] = back[2 * m + 1].astype(BF16)
    weights[...] = lax.dot_general(
        agg[...], grads[...], ROWS_ROWS, preferred_element_type=F32
    ).reshape(weights.shape)
    core = me_row % 2
    after = n_row // 2 * side
    kept_weight[...] = weights[core]
    sent[after : after + half] = weights[1 - core].astype(BF16)
    column_sum = jnp.sum(grads[...].astype(F32), axis=0, keepdims=True)
    sent[after + half : after + half + PAD] = two_halves(column_sum)


def chip_kernel(kept, kept_weight, own_sent, came, mine, *outs):
    half, side = kept_weight.shape[0], mine.shape[0]
    after = kept.shape[0]
    mine[...] = kept[0:side] + came[0:side].astype(F32)
    weights = (kept_weight[...] + came[after : after + half].astype(F32)).astype(BF16)
    ends = slice(after + half, after + half + PAD)
    column_sum = two_halves(joined(own_sent[ends]) + joined(came[ends]))
    for m, out in enumerate(outs, 1):
        part = slice(m * side, (m + 1) * side)
        out[0:side] = (kept[part] + came[part].astype(F32)).astype(BF16)
        out[side : side + half] = weights
        out[side + half : side + half + PAD] = column_sum


def line_kernel(scale, own_hidden, mine, *refs):
    blocks, (hidden, grad_features, grad_weight, grad_bias) = refs[:-4], refs[-4:]
    hidden[...] = own_hidden[...]
    side, half = mine.shape[0], grad_weight.shape[0] // 2
    own, other = blocks[: len(blocks) // 2], blocks[len(blocks) // 2 :]
    total = mine[...]
    for block in own[1:]:
        total = total + block[0:side].astype(F32)
    grad_features[...] = total.astype(BF16)
    for shift, group in enumerate((own, other)):
        start = pl.multiple_of((lax.axis_index("row") % 2 ^ shift) * half, half)
        grad_weight[pl.ds(start, half), :] = scale * tree_sum(
            b[side : side + half].astype(F32) for b in group
        )
    grad_bias[...] = scale * tree_sum(joined(b[side + half : side + half + PAD]) for b in own)


def call(kernel, name, outs, scratch, ints, *arrays):
    need = sum(math.prod(shape) * jnp.dtype(dtype).itemsize for shape, dtype in scratch)

    def space(dtype):
        return pltpu.SMEM if dtype == jnp.int32 else pltpu.VMEM

    return pl.pallas_call(
        kernel,
        name=name,
        out_shape=[
            space(dtype)(shape, dtype) if stays else jax.ShapeDtypeStruct(shape, dtype)
            for shape, dtype, stays in outs
        ],
        in_specs=[pl.BlockSpec(memory_space=pltpu.SMEM)] * len(ints)
        + [pl.BlockSpec(memory_space=pltpu.VMEM)] * len(arrays),
        out_specs=[pl.BlockSpec(memory_space=space(dtype)) for _, dtype, _ in outs],
        scratch_shapes=[space(dtype)(shape, dtype) for shape, dtype in scratch],
        compiler_params=pltpu.CompilerParams(vmem_limit_bytes=need + 8 * 1024 * 1024),
    )(*ints, *arrays)


def near(array):
    return pltpu.with_memory_space_constraint(array, pltpu.VMEM)


def far(array):
    return pltpu.with_memory_space_constraint(array, pltpu.HBM)


def on_device(
    features, tiles, tile_rows, tile_cols, tile_count, weight, bias, cotangent, label_mask
):
    side = tiles.shape[-1]
    slots = tiles.shape[2]
    width = features.shape[2]
    n_row = lax.axis_size("row")
    n_col = lax.axis_size("col")
    n_line = n_row // 2
    blocks = min(slots, n_col)
    own_tiles = near(tiles[0, 0])

    own = features[0]
    along = [own] + [exchange(own, "row", 2 * m) for m in range(1, n_line)]

    with_places, own_bias, ints = call(
        functools.partial(cotangent_kernel, blocks),
        "masked_cotangent",
        [((side + blocks + -blocks % PAD, width), BF16, True), ((1, width), F32, True), ((2 * slots,), jnp.int32, True)],
        [],
        [far(tile_rows[0, 0]), far(tile_cols[0, 0])],
        far(label_mask),
        far(cotangent[0]),
        far(bias[None]),
    )
    ints = pltpu.with_memory_space_constraint(ints, pltpu.SMEM)
    cots, reach = [with_places], 1
    while reach < n_col:
        (held,) = call(
            stack_kernel,
            "cotangents_so_far",
            [((reach * with_places.shape[0], width), BF16, True)],
            [],
            [],
            *map(near, cots),
        ) if reach > 1 else cots
        cots, reach = cots + [exchange(held, "col", reach)], 2 * reach

    sources = [own, exchange(own, "row", 1)]
    tile_count, _ = lax.optimization_barrier((tile_count, sources[1]))
    counts = jnp.broadcast_to(tile_count, (8, 128))
    for block in along[1:]:
        block, _ = lax.optimization_barrier((block, counts))
        sources += [block, exchange(block, "row", 1)]
    product, count = call(
        functools.partial(forward_kernel, slots, n_col, blocks),
        "tile_products",
        [((blocks * side, width), BF16, True), ((2,), jnp.int32, True)],
        [((n_row, side, width), BF16), ((n_col, side, width), F32)],
        [ints],
        near(counts),
        own_tiles,
        *map(near, sources),
    )
    products = lax.all_gather(product, "col")
    after = n_line * side
    half = width // 2
    hidden, sent, kept_back, kept_weight = call(
        functools.partial(middle_kernel, slots, n_row, n_col, blocks),
        "dense_layer",
        [
            ((side, width), BF16, True),
            ((after + half + PAD, width), BF16, True),
            ((after, width), F32, True),
            ((half, width), F32, True),
        ],
        [
            ((n_col, side, width), F32),
            ((n_col * side, width), BF16),
            ((n_col * side, width), BF16),
            ((n_col, side, width), BF16),
            ((2, half, width), F32),
            ((n_row, side, width), F32),
            ((n_col, blocks), jnp.int32),
        ],
        [ints, pltpu.with_memory_space_constraint(count, pltpu.SMEM)],
        near(weight),
        near(own_bias),
        own_tiles,
        near(products),
        *map(near, cots),
    )
    came = exchange(sent, "row", 1)
    mine, *parts = call(
        chip_kernel,
        "chip_sums",
        [((side, width), F32, True)] + [((side + half + PAD, width), BF16, True)] * (n_line - 1),
        [],
        [],
        *map(near, (kept_back, kept_weight, sent, came)),
    )
    line = [parts[0]] + [exchange(part, "row", 2 * m) for m, part in enumerate(parts, 1)]
    other = [exchange(block, "row", 1) for block in line]
    scale = 1.0 / math.sqrt(n_row * n_col * side)
    hidden, grad_features, grad_weight, grad_bias = call(
        functools.partial(line_kernel, scale),
        "line_sums",
        [
            ((side, width), BF16, False),
            ((side, width), BF16, False),
            ((width, width), F32, False),
            ((1, width), F32, False),
        ],
        [],
        [],
        *map(near, (hidden, mine, *line, *other)),
    )
    return (hidden[None], grad_weight, grad_bias[0], grad_features[None])


def solution(mesh):
    return jax.shard_map(
        on_device,
        mesh=mesh,
        in_specs=(
            P("col", "row", None),
            P("row", "col", None, None, None),
            P("row", "col", None),
            P("row", "col", None),
            P("row", "col"),
            P(),
            P(),
            P("row", "col", None),
            P("row", "col"),
        ),
        out_specs=(P("row", "col", None), P(), P(), P("col", "row", None)),
        check_vma=False,
    )
```

```python
import functools
import math

import jax
import jax.numpy as jnp
from jax import lax
from jax.experimental import pallas as pl
from jax.experimental.pallas import tpu as pltpu
from jax.sharding import PartitionSpec as P

F32 = jnp.float32
BF16 = jnp.bfloat16
PAD = 16
ROWS_ROWS = (((0,), (0,)), ((), ()))
COLS_COLS = (((1,), (1,)), ((), ()))


def each(count, body):
    if count <= 16:
        for i in range(count):
            body(i)
    else:
        lax.fori_loop(0, count, lambda i, carry: (body(i), carry)[1], 0)


def exchange(value, axis, mask):
    size = lax.axis_size(axis)
    return lax.ppermute(value, axis, [(i, i ^ mask) for i in range(size)])


def tree_sum(terms):
    terms = list(terms)
    while len(terms) > 1:
        terms = [a + b for a, b in zip(terms[::2], terms[1::2], strict=True)]
    return terms[0]


def two_halves(row):
    high = row.astype(BF16)
    low = (row - high.astype(F32)).astype(BF16)
    place = lax.broadcasted_iota(jnp.int32, (PAD, row.shape[-1]), 0)
    block = jnp.where(place == 0, high.astype(F32), jnp.where(place == 1, low.astype(F32), 0.0))
    return block.astype(BF16)


def joined(block):
    rows = block.astype(F32)
    return rows[0:1] + rows[1:2]


def cotangent_kernel(blocks, tile_rows, tile_cols, mask, cotangent, bias, out, own_bias, ints):
    own_bias[...] = bias[...]
    slots = tile_rows.shape[0]
    for s in range(slots):
        ints[s] = tile_rows[s]
        ints[slots + s] = tile_cols[s]
    side, width = cotangent.shape
    shape = (side, side)
    diagonal = lax.broadcasted_iota(jnp.int32, shape, 0) == lax.broadcasted_iota(jnp.int32, shape, 1)
    spread = jnp.where(diagonal, mask[...].astype(F32), 0.0).astype(BF16)
    out[0:side] = jnp.dot(spread, cotangent[...], preferred_element_type=F32).astype(BF16)
    rows = out.shape[0] - side
    index = lax.broadcasted_iota(jnp.int32, (rows, width), 0)
    block = jnp.zeros((rows, width), jnp.int32)
    for p in range(blocks):
        block = jnp.where(index == p, tile_rows[p] if blocks == slots else p, block)
    out[side:] = block.astype(F32).astype(BF16)


def stack_kernel(*refs):
    out, start = refs[-1], 0
    for block in refs[:-1]:
        out[start : start + block.shape[0]] = block[...]
        start += block.shape[0]


def forward_kernel(slots, n_col, blocks, ints, counts, tiles, *refs):
    n_row = len(refs) - 4
    sources, (out, count, held, total) = refs[:n_row], refs[n_row:]
    count[0] = jnp.max(counts[...])
    side = tiles.shape[-1]
    for q in range(n_row):
        held[q] = sources[q][...]
    me_row, live = lax.axis_index("row"), count[0]

    def product(s):
        taken = held[ints[slots + s] ^ me_row]
        value = jnp.dot(tiles[s], taken, preferred_element_type=F32)
        return jnp.where(s < live, value, 0.0)

    if blocks == slots:
        for s in range(slots):
            out[s * side : (s + 1) * side] = product(s).astype(BF16)
        return
    total[...] = jnp.zeros_like(total)

    def add(s):
        total[ints[s]] += product(s)

    each(slots, add)
    for t in range(n_col):
        out[t * side : (t + 1) * side] = total[t].astype(BF16)


def middle_kernel(slots, n_row, n_col, blocks, *refs):
    (ints, count), refs = refs[:2], refs[2:]
    (weight, bias, tiles, products), refs = refs[:4], refs[4:]
    steps = n_col.bit_length()
    cots, refs = refs[:steps], refs[steps:]
    hidden, sent, kept, kept_weight, total, agg, grads, grad_agg, weights, back, target = refs
    side = tiles.shape[-1]
    half = weight.shape[0] // 2
    me_row, me_col, live = lax.axis_index("row"), lax.axis_index("col"), count[0]
    each_rows = cots[0].shape[0]

    def cotangent(q, start, stop):
        step = q.bit_length()
        first = (q - (1 << step >> 1)) * each_rows
        return cots[step][first + start : first + stop]

    for q in range(n_col):
        places = cotangent(q, side, each_rows)[:, 0:128].astype(F32).astype(jnp.int32)
        for p in range(blocks):
            target[q, p] = jnp.max(places[p : p + 1])
    total[...] = jnp.zeros_like(total)

    def add(i):
        c, p = i // blocks, i % blocks
        q = me_col ^ c
        total[target[q, p]] += products[c, pl.ds(p * side, side), :].astype(F32)

    each(n_col * blocks, add)
    for q in range(n_col):
        t = me_col ^ q
        rows = pl.ds(pl.multiple_of(t * side, side), side)
        aggregated = total[t].astype(BF16)
        agg[rows, :] = aggregated
        pre_act = jnp.dot(aggregated, weight[...], preferred_element_type=F32) + bias[...]
        sigma = jax.nn.sigmoid(pre_act)
        if q == 0:
            hidden[...] = (pre_act * sigma).astype(BF16)
        slope = sigma * (1.0 + pre_act * (1.0 - sigma))
        grad_pre = (cotangent(q, 0, side).astype(F32) * slope).astype(BF16)
        grads[rows, :] = grad_pre
        grad_agg[t] = lax.dot_general(
            grad_pre, weight[...], COLS_COLS, preferred_element_type=F32
        ).astype(BF16)
    back[...] = jnp.zeros_like(back)

    def put(s):
        value = lax.dot_general(
            tiles[s], grad_agg[ints[s]], ROWS_ROWS, preferred_element_type=F32
        )
        back[ints[slots + s] ^ me_row] += jnp.where(s < live, value, 0.0)

    each(slots, put)
    for m in range(n_row // 2):
        kept[m * side : (m + 1) * side] = back[2 * m]
        sent[m * side : (m + 1) * side] = back[2 * m + 1].astype(BF16)
    weights[...] = lax.dot_general(
        agg[...], grads[...], ROWS_ROWS, preferred_element_type=F32
    ).reshape(weights.shape)
    core = me_row % 2
    after = n_row // 2 * side
    kept_weight[...] = weights[core]
    sent[after : after + half] = weights[1 - core].astype(BF16)
    column_sum = jnp.sum(grads[...].astype(F32), axis=0, keepdims=True)
    sent[after + half : after + half + PAD] = two_halves(column_sum)


def chip_kernel(kept, kept_weight, own_sent, came, mine, *outs):
    half, side = kept_weight.shape[0], mine.shape[0]
    after = kept.shape[0]
    mine[...] = kept[0:side] + came[0:side].astype(F32)
    weights = (kept_weight[...] + came[after : after + half].astype(F32)).astype(BF16)
    ends = slice(after + half, after + half + PAD)
    column_sum = two_halves(joined(own_sent[ends]) + joined(came[ends]))
    for m, out in enumerate(outs, 1):
        part = slice(m * side, (m + 1) * side)
        out[0:side] = (kept[part] + came[part].astype(F32)).astype(BF16)
        out[side : side + half] = weights
        out[side + half : side + half + PAD] = column_sum


def line_weight_kernel(scale, *refs):
    blocks, out = refs[:-1], refs[-1]
    half = out.shape[0] - 8
    start = blocks[0].shape[0] - half - PAD
    out[0:half] = scale * tree_sum(b[start : start + half].astype(F32) for b in blocks)
    column_sum = scale * tree_sum(joined(b[start + half :]) for b in blocks)
    out[half:] = jnp.broadcast_to(column_sum, (8, column_sum.shape[1]))


def node_results_kernel(own_hidden, mine, *refs):
    blocks, (hidden, grad_features) = refs[:-2], refs[-2:]
    hidden[...] = own_hidden[...]
    side = mine.shape[0]
    total = mine[...]
    for block in blocks:
        total = total + block[0:side].astype(F32)
    grad_features[...] = total.astype(BF16)


def weight_results_kernel(own, other, grad_weight, grad_bias):
    half = grad_weight.shape[0] // 2
    for shift, block in enumerate((own, other)):
        start = pl.multiple_of((lax.axis_index("row") % 2 ^ shift) * half, half)
        grad_weight[pl.ds(start, half), :] = block[0:half]
    grad_bias[...] = own[half : half + 1]


def call(kernel, name, outs, scratch, ints, *arrays):
    need = sum(math.prod(shape) * jnp.dtype(dtype).itemsize for shape, dtype in scratch)

    def space(dtype):
        return pltpu.SMEM if dtype == jnp.int32 else pltpu.VMEM

    return pl.pallas_call(
        kernel,
        name=name,
        out_shape=[
            space(dtype)(shape, dtype) if stays else jax.ShapeDtypeStruct(shape, dtype)
            for shape, dtype, stays in outs
        ],
        in_specs=[pl.BlockSpec(memory_space=pltpu.SMEM)] * len(ints)
        + [pl.BlockSpec(memory_space=pltpu.VMEM)] * len(arrays),
        out_specs=[pl.BlockSpec(memory_space=space(dtype)) for _, dtype, _ in outs],
        scratch_shapes=[space(dtype)(shape, dtype) for shape, dtype in scratch],
        compiler_params=pltpu.CompilerParams(vmem_limit_bytes=need + 8 * 1024 * 1024),
    )(*ints, *arrays)


def near(array):
    return pltpu.with_memory_space_constraint(array, pltpu.VMEM)


def far(array):
    return pltpu.with_memory_space_constraint(array, pltpu.HBM)


def on_device(
    features, tiles, tile_rows, tile_cols, tile_count, weight, bias, cotangent, label_mask
):
    side = tiles.shape[-1]
    slots = tiles.shape[2]
    width = features.shape[2]
    n_row = lax.axis_size("row")
    n_col = lax.axis_size("col")
    n_line = n_row // 2
    blocks = min(slots, n_col)
    own_tiles = near(tiles[0, 0])

    own = features[0]
    along = [own] + [exchange(own, "row", 2 * m) for m in range(1, n_line)]

    with_places, own_bias, ints = call(
        functools.partial(cotangent_kernel, blocks),
        "masked_cotangent",
        [((side + blocks + -blocks % PAD, width), BF16, True), ((1, width), F32, True), ((2 * slots,), jnp.int32, True)],
        [],
        [far(tile_rows[0, 0]), far(tile_cols[0, 0])],
        far(label_mask),
        far(cotangent[0]),
        far(bias[None]),
    )
    ints = pltpu.with_memory_space_constraint(ints, pltpu.SMEM)
    cots, reach = [with_places], 1
    while reach < n_col:
        (held,) = call(
            stack_kernel,
            "cotangents_so_far",
            [((reach * with_places.shape[0], width), BF16, True)],
            [],
            [],
            *map(near, cots),
        ) if reach > 1 else cots
        cots, reach = cots + [exchange(held, "col", reach)], 2 * reach

    sources = [own, exchange(own, "row", 1)]
    tile_count, _ = lax.optimization_barrier((tile_count, sources[1]))
    counts = jnp.broadcast_to(tile_count, (8, 128))
    for block in along[1:]:
        block, _ = lax.optimization_barrier((block, counts))
        sources += [block, exchange(block, "row", 1)]
    product, count = call(
        functools.partial(forward_kernel, slots, n_col, blocks),
        "tile_products",
        [((blocks * side, width), BF16, True), ((2,), jnp.int32, True)],
        [((n_row, side, width), BF16), ((n_col, side, width), F32)],
        [ints],
        near(counts),
        own_tiles,
        *map(near, sources),
    )
    products = lax.all_gather(product, "col")
    after = n_line * side
    half = width // 2
    hidden, sent, kept_back, kept_weight = call(
        functools.partial(middle_kernel, slots, n_row, n_col, blocks),
        "dense_layer",
        [
            ((side, width), BF16, True),
            ((after + half + PAD, width), BF16, True),
            ((after, width), F32, True),
            ((half, width), F32, True),
        ],
        [
            ((n_col, side, width), F32),
            ((n_col * side, width), BF16),
            ((n_col * side, width), BF16),
            ((n_col, side, width), BF16),
            ((2, half, width), F32),
            ((n_row, side, width), F32),
            ((n_col, blocks), jnp.int32),
        ],
        [ints, pltpu.with_memory_space_constraint(count, pltpu.SMEM)],
        near(weight),
        near(own_bias),
        own_tiles,
        near(products),
        *map(near, cots),
    )
    came = exchange(sent, "row", 1)
    mine, *parts = call(
        chip_kernel,
        "chip_sums",
        [((side, width), F32, True)] + [((side + half + PAD, width), BF16, True)] * (n_line - 1),
        [],
        [],
        *map(near, (kept_back, kept_weight, sent, came)),
    )
    line = [parts[0]] + [exchange(part, "row", 2 * m) for m, part in enumerate(parts, 1)]
    scale = 1.0 / math.sqrt(n_row * n_col * side)
    (weights,) = call(
        functools.partial(line_weight_kernel, scale),
        "line_weight",
        [((half + 8, width), F32, True)],
        [],
        [],
        *map(near, line),
    )
    other_weights = exchange(weights, "row", 1)
    hidden, grad_features = call(
        node_results_kernel,
        "node_results",
        [((side, width), BF16, False), ((side, width), BF16, False)],
        [],
        [],
        *map(near, (hidden, mine, *line[1:])),
    )
    grad_weight, grad_bias = call(
        weight_results_kernel,
        "weight_results",
        [((width, width), F32, False), ((1, width), F32, False)],
        [],
        [],
        near(weights),
        near(other_weights),
    )
    return (hidden[None], grad_weight, grad_bias[0], grad_features[None])


def solution(mesh):
    return jax.shard_map(
        on_device,
        mesh=mesh,
        in_specs=(
            P("col", "row", None),
            P("row", "col", None, None, None),
            P("row", "col", None),
            P("row", "col", None),
            P("row", "col"),
            P(),
            P(),
            P("row", "col", None),
            P("row", "col"),
        ),
        out_specs=(P("row", "col", None), P(), P(), P("col", "row", None)),
        check_vma=False,
    )
```

```python
import functools
import math

import jax
import jax.numpy as jnp
from jax import lax
from jax.experimental import pallas as pl
from jax.experimental.pallas import tpu as pltpu
from jax.sharding import PartitionSpec as P

F32 = jnp.float32
BF16 = jnp.bfloat16
PAD = 16
ROWS_ROWS = (((0,), (0,)), ((), ()))
COLS_COLS = (((1,), (1,)), ((), ()))


def each(count, body):
    if count <= 16:
        for i in range(count):
            body(i)
    else:
        lax.fori_loop(0, count, lambda i, carry: (body(i), carry)[1], 0)


def exchange(value, axis, mask):
    size = lax.axis_size(axis)
    return lax.ppermute(value, axis, [(i, i ^ mask) for i in range(size)])


def column_mask(core, q, n_col):
    if n_col < 4 or core == 0:
        return q
    return q - q % 4 + (0, 2, 1, 3)[q % 4]


def column_exchange(value, q):
    rows, cols = lax.axis_size("row"), lax.axis_size("col")
    pairs = [(r * cols + c, r * cols + (c ^ column_mask(r % 2, q, cols))) for r in range(rows) for c in range(cols)]
    return lax.ppermute(value, ("row", "col"), pairs)


def line_mask(core, m, n_line):
    if n_line < 4 or core == 0:
        return m
    return m - m % 4 + (0, 1, 3, 2)[m % 4]


def line_exchange(value, m):
    size = lax.axis_size("row")
    pairs = [(i, i ^ 2 * line_mask(i % 2, m, size // 2)) for i in range(size)]
    return lax.ppermute(value, "row", pairs)


def tree_sum(terms):
    terms = list(terms)
    while len(terms) > 1:
        terms = [a + b for a, b in zip(terms[::2], terms[1::2], strict=True)]
    return terms[0]


def two_halves(row):
    high = row.astype(BF16)
    low = (row - high.astype(F32)).astype(BF16)
    place = lax.broadcasted_iota(jnp.int32, (PAD, row.shape[-1]), 0)
    block = jnp.where(place == 0, high.astype(F32), jnp.where(place == 1, low.astype(F32), 0.0))
    return block.astype(BF16)


def joined(block):
    rows = block.astype(F32)
    return rows[0:1] + rows[1:2]


def cotangent_kernel(blocks, tile_rows, tile_cols, mask, cotangent, bias, out, own_bias, ints):
    own_bias[...] = bias[...]
    slots = tile_rows.shape[0]
    for s in range(slots):
        ints[s] = tile_rows[s]
        ints[slots + s] = tile_cols[s]
    side, width = cotangent.shape
    shape = (side, side)
    diagonal = lax.broadcasted_iota(jnp.int32, shape, 0) == lax.broadcasted_iota(jnp.int32, shape, 1)
    spread = jnp.where(diagonal, mask[...].astype(F32), 0.0).astype(BF16)
    out[0:side] = jnp.dot(spread, cotangent[...], preferred_element_type=F32).astype(BF16)
    rows = out.shape[0] - side
    index = lax.broadcasted_iota(jnp.int32, (rows, width), 0)
    block = jnp.zeros((rows, width), jnp.int32)
    for p in range(blocks):
        block = jnp.where(index == p, tile_rows[p] if blocks == slots else p, block)
    out[side:] = block.astype(F32).astype(BF16)


def stack_kernel(*refs):
    out, start = refs[-1], 0
    for block in refs[:-1]:
        out[start : start + block.shape[0]] = block[...]
        start += block.shape[0]


def forward_kernel(slots, n_col, blocks, ints, counts, tiles, *refs):
    n_row = len(refs) - 4
    sources, (out, count, held, total) = refs[:n_row], refs[n_row:]
    count[0] = jnp.max(counts[...])
    side = tiles.shape[-1]
    for q in range(n_row):
        held[q] = sources[q][...]
    me_row, live = lax.axis_index("row"), count[0]

    def product(s):
        taken = held[ints[slots + s] ^ me_row]
        value = jnp.dot(tiles[s], taken, preferred_element_type=F32)
        return jnp.where(s < live, value, 0.0)

    if blocks == slots:
        for s in range(slots):
            out[s * side : (s + 1) * side] = product(s).astype(BF16)
        return
    total[...] = jnp.zeros_like(total)

    def add(s):
        total[ints[s]] += product(s)

    each(slots, add)
    for t in range(n_col):
        out[t * side : (t + 1) * side] = total[t].astype(BF16)


def middle_kernel(slots, n_row, n_col, blocks, *refs):
    (ints, count), refs = refs[:2], refs[2:]
    (weight, bias, tiles, products), refs = refs[:4], refs[4:]
    steps = n_col.bit_length()
    cots, refs = refs[:steps], refs[steps:]
    hidden, sent, kept, kept_weight, total, agg, grads, grad_agg, weights, back, target = refs
    side = tiles.shape[-1]
    half = weight.shape[0] // 2
    me_row, me_col, live = lax.axis_index("row"), lax.axis_index("col"), count[0]
    each_rows = cots[0].shape[0]

    def cotangent(q, start, stop):
        step = q.bit_length()
        first = (q - (1 << step >> 1)) * each_rows
        return cots[step][first + start : first + stop]

    second = me_row % 2
    places_of = [
        me_col ^ jnp.where(second == 1, column_mask(1, q, n_col), column_mask(0, q, n_col))
        for q in range(n_col)
    ]
    for q in range(n_col):
        places = cotangent(q, side, each_rows)[:, 0:128].astype(F32).astype(jnp.int32)
        for p in range(blocks):
            target[places_of[q], p] = jnp.max(places[p : p + 1])
    total[...] = jnp.zeros_like(total)

    def add(i):
        c, p = i // blocks, i % blocks
        total[target[c, p]] += products[c, pl.ds(p * side, side), :].astype(F32)

    each(n_col * blocks, add)
    for q in range(n_col):
        t = places_of[q]
        rows = pl.ds(pl.multiple_of(t * side, side), side)
        aggregated = total[t].astype(BF16)
        agg[rows, :] = aggregated
        pre_act = jnp.dot(aggregated, weight[...], preferred_element_type=F32) + bias[...]
        sigma = jax.nn.sigmoid(pre_act)
        if q == 0:
            hidden[...] = (pre_act * sigma).astype(BF16)
        slope = sigma * (1.0 + pre_act * (1.0 - sigma))
        grad_pre = (cotangent(q, 0, side).astype(F32) * slope).astype(BF16)
        grads[rows, :] = grad_pre
        grad_agg[t] = lax.dot_general(
            grad_pre, weight[...], COLS_COLS, preferred_element_type=F32
        ).astype(BF16)
    back[...] = jnp.zeros_like(back)

    def put(s):
        value = lax.dot_general(
            tiles[s], grad_agg[ints[s]], ROWS_ROWS, preferred_element_type=F32
        )
        back[ints[slots + s] ^ me_row] += jnp.where(s < live, value, 0.0)

    each(slots, put)
    for m in range(n_row // 2):
        kept[m * side : (m + 1) * side] = back[2 * m]
        sent[m * side : (m + 1) * side] = back[2 * m + 1].astype(BF16)
    weights[...] = lax.dot_general(
        agg[...], grads[...], ROWS_ROWS, preferred_element_type=F32
    ).reshape(weights.shape)
    core = me_row % 2
    after = n_row // 2 * side
    kept_weight[...] = weights[core]
    sent[after : after + half] = weights[1 - core].astype(BF16)
    column_sum = jnp.sum(grads[...].astype(F32), axis=0, keepdims=True)
    sent[after + half : after + half + PAD] = two_halves(column_sum)


def chip_kernel(kept, kept_weight, own_sent, came, mine, *outs):
    half, side = kept_weight.shape[0], mine.shape[0]
    after = kept.shape[0]
    mine[...] = kept[0:side] + came[0:side].astype(F32)
    weights = (kept_weight[...] + came[after : after + half].astype(F32)).astype(BF16)
    ends = slice(after + half, after + half + PAD)
    column_sum = two_halves(joined(own_sent[ends]) + joined(came[ends]))
    n_line, second = len(outs) + 1, lax.axis_index("row") % 2
    for m, out in enumerate(outs, 1):
        chosen = jnp.where(second == 1, line_mask(1, m, n_line), line_mask(0, m, n_line))
        part = pl.ds(pl.multiple_of(chosen * side, side), side)
        out[0:side] = (kept[part, :] + came[part, :].astype(F32)).astype(BF16)
        out[side : side + half] = weights
        out[side + half : side + half + PAD] = column_sum


def line_weight_kernel(scale, *refs):
    blocks, out = refs[:-1], refs[-1]
    half = out.shape[0] - 8
    start = blocks[0].shape[0] - half - PAD
    out[0:half] = scale * tree_sum(b[start : start + half].astype(F32) for b in blocks)
    column_sum = scale * tree_sum(joined(b[start + half :]) for b in blocks)
    out[half:] = jnp.broadcast_to(column_sum, (8, column_sum.shape[1]))


def node_results_kernel(own_hidden, mine, *refs):
    blocks, (hidden, grad_features) = refs[:-2], refs[-2:]
    hidden[...] = own_hidden[...]
    side = mine.shape[0]
    total = mine[...]
    for block in blocks:
        total = total + block[0:side].astype(F32)
    grad_features[...] = total.astype(BF16)


def weight_results_kernel(own, other, grad_weight, grad_bias):
    half = grad_weight.shape[0] // 2
    for shift, block in enumerate((own, other)):
        start = pl.multiple_of((lax.axis_index("row") % 2 ^ shift) * half, half)
        grad_weight[pl.ds(start, half), :] = block[0:half]
    grad_bias[...] = own[half : half + 1]


def call(kernel, name, outs, scratch, ints, *arrays):
    need = sum(math.prod(shape) * jnp.dtype(dtype).itemsize for shape, dtype in scratch)

    def space(dtype):
        return pltpu.SMEM if dtype == jnp.int32 else pltpu.VMEM

    return pl.pallas_call(
        kernel,
        name=name,
        out_shape=[
            space(dtype)(shape, dtype) if stays else jax.ShapeDtypeStruct(shape, dtype)
            for shape, dtype, stays in outs
        ],
        in_specs=[pl.BlockSpec(memory_space=pltpu.SMEM)] * len(ints)
        + [pl.BlockSpec(memory_space=pltpu.VMEM)] * len(arrays),
        out_specs=[pl.BlockSpec(memory_space=space(dtype)) for _, dtype, _ in outs],
        scratch_shapes=[space(dtype)(shape, dtype) for shape, dtype in scratch],
        compiler_params=pltpu.CompilerParams(vmem_limit_bytes=need + 8 * 1024 * 1024),
    )(*ints, *arrays)


def near(array):
    return pltpu.with_memory_space_constraint(array, pltpu.VMEM)


def far(array):
    return pltpu.with_memory_space_constraint(array, pltpu.HBM)


def on_device(
    features, tiles, tile_rows, tile_cols, tile_count, weight, bias, cotangent, label_mask
):
    side = tiles.shape[-1]
    slots = tiles.shape[2]
    width = features.shape[2]
    n_row = lax.axis_size("row")
    n_col = lax.axis_size("col")
    n_line = n_row // 2
    blocks = min(slots, n_col)
    own_tiles = near(tiles[0, 0])

    own = features[0]
    along = [own] + [exchange(own, "row", 2 * m) for m in range(1, n_line)]

    with_places, own_bias, ints = call(
        functools.partial(cotangent_kernel, blocks),
        "masked_cotangent",
        [((side + blocks + -blocks % PAD, width), BF16, True), ((1, width), F32, True), ((2 * slots,), jnp.int32, True)],
        [],
        [far(tile_rows[0, 0]), far(tile_cols[0, 0])],
        far(label_mask),
        far(cotangent[0]),
        far(bias[None]),
    )
    ints = pltpu.with_memory_space_constraint(ints, pltpu.SMEM)
    cots, reach = [with_places], 1
    while reach < n_col:
        (held,) = call(
            stack_kernel,
            "cotangents_so_far",
            [((reach * with_places.shape[0], width), BF16, True)],
            [],
            [],
            *map(near, cots),
        ) if reach > 1 else cots
        cots, reach = cots + [column_exchange(held, reach)], 2 * reach

    sources = [own, exchange(own, "row", 1)]
    tile_count, _ = lax.optimization_barrier((tile_count, sources[1]))
    counts = jnp.broadcast_to(tile_count, (8, 128))
    for block in along[1:]:
        block, _ = lax.optimization_barrier((block, counts))
        sources += [block, exchange(block, "row", 1)]
    product, count = call(
        functools.partial(forward_kernel, slots, n_col, blocks),
        "tile_products",
        [((blocks * side, width), BF16, True), ((2,), jnp.int32, True)],
        [((n_row, side, width), BF16), ((n_col, side, width), F32)],
        [ints],
        near(counts),
        own_tiles,
        *map(near, sources),
    )
    products = lax.all_gather(product, "col")
    after = n_line * side
    half = width // 2
    hidden, sent, kept_back, kept_weight = call(
        functools.partial(middle_kernel, slots, n_row, n_col, blocks),
        "dense_layer",
        [
            ((side, width), BF16, True),
            ((after + half + PAD, width), BF16, True),
            ((after, width), F32, True),
            ((half, width), F32, True),
        ],
        [
            ((n_col, side, width), F32),
            ((n_col * side, width), BF16),
            ((n_col * side, width), BF16),
            ((n_col, side, width), BF16),
            ((2, half, width), F32),
            ((n_row, side, width), F32),
            ((n_col, blocks), jnp.int32),
        ],
        [ints, pltpu.with_memory_space_constraint(count, pltpu.SMEM)],
        near(weight),
        near(own_bias),
        own_tiles,
        near(products),
        *map(near, cots),
    )
    came = exchange(sent, "row", 1)
    mine, *parts = call(
        chip_kernel,
        "chip_sums",
        [((side, width), F32, True)] + [((side + half + PAD, width), BF16, True)] * (n_line - 1),
        [],
        [],
        *map(near, (kept_back, kept_weight, sent, came)),
    )
    line = [parts[0]] + [line_exchange(part, m) for m, part in enumerate(parts, 1)]
    scale = 1.0 / math.sqrt(n_row * n_col * side)
    (weights,) = call(
        functools.partial(line_weight_kernel, scale),
        "line_weight",
        [((half + 8, width), F32, True)],
        [],
        [],
        *map(near, line),
    )
    other_weights = exchange(weights, "row", 1)
    hidden, grad_features = call(
        node_results_kernel,
        "node_results",
        [((side, width), BF16, False), ((side, width), BF16, False)],
        [],
        [],
        *map(near, (hidden, mine, *line[1:])),
    )
    grad_weight, grad_bias = call(
        weight_results_kernel,
        "weight_results",
        [((width, width), F32, False), ((1, width), F32, False)],
        [],
        [],
        near(weights),
        near(other_weights),
    )
    return (hidden[None], grad_weight, grad_bias[0], grad_features[None])


def solution(mesh):
    return jax.shard_map(
        on_device,
        mesh=mesh,
        in_specs=(
            P("col", "row", None),
            P("row", "col", None, None, None),
            P("row", "col", None),
            P("row", "col", None),
            P("row", "col"),
            P(),
            P(),
            P("row", "col", None),
            P("row", "col"),
        ),
        out_specs=(P("row", "col", None), P(), P(), P("col", "row", None)),
        check_vma=False,
    )
```

```python
import functools
import math

import jax
import jax.numpy as jnp
from jax import lax
from jax.experimental import pallas as pl
from jax.experimental.pallas import tpu as pltpu
from jax.sharding import PartitionSpec as P

F32 = jnp.float32
BF16 = jnp.bfloat16
PAD = 16
ROWS_ROWS = (((0,), (0,)), ((), ()))
COLS_COLS = (((1,), (1,)), ((), ()))


def each(count, body):
    if count <= 16:
        for i in range(count):
            body(i)
    else:
        lax.fori_loop(0, count, lambda i, carry: (body(i), carry)[1], 0)


def exchange(value, axis, mask):
    size = lax.axis_size(axis)
    return lax.ppermute(value, axis, [(i, i ^ mask) for i in range(size)])


def column_mask(core, q, n_col):
    if n_col < 4 or core == 0:
        return q
    return q - q % 4 + (0, 2, 1, 3)[q % 4]


def column_exchange(value, q):
    rows, cols = lax.axis_size("row"), lax.axis_size("col")
    pairs = [(r * cols + c, r * cols + (c ^ column_mask(r % 2, q, cols))) for r in range(rows) for c in range(cols)]
    return lax.ppermute(value, ("row", "col"), pairs)


def line_mask(core, m, n_line):
    if n_line < 4 or core == 0:
        return m
    return m - m % 4 + (0, 1, 3, 2)[m % 4]


def carries_bias(m, n_line):
    return n_line < 4 or m % 4 != 3


def line_exchange(value, m):
    size = lax.axis_size("row")
    pairs = [(i, i ^ 2 * line_mask(i % 2, m, size // 2)) for i in range(size)]
    return lax.ppermute(value, "row", pairs)


def tree_sum(terms):
    terms = list(terms)
    while len(terms) > 1:
        terms = [a + b for a, b in zip(terms[::2], terms[1::2], strict=True)]
    return terms[0]


def two_halves(row):
    high = row.astype(BF16)
    low = (row - high.astype(F32)).astype(BF16)
    place = lax.broadcasted_iota(jnp.int32, (PAD, row.shape[-1]), 0)
    block = jnp.where(place == 0, high.astype(F32), jnp.where(place == 1, low.astype(F32), 0.0))
    return block.astype(BF16)


def joined(block):
    rows = block.astype(F32)
    return rows[0:1] + rows[1:2]


def cotangent_kernel(blocks, tile_rows, tile_cols, mask, cotangent, bias, out, own_bias, ints):
    own_bias[...] = bias[...]
    slots = tile_rows.shape[0]
    for s in range(slots):
        ints[s] = tile_rows[s]
        ints[slots + s] = tile_cols[s]
    side, width = cotangent.shape
    shape = (side, side)
    diagonal = lax.broadcasted_iota(jnp.int32, shape, 0) == lax.broadcasted_iota(jnp.int32, shape, 1)
    spread = jnp.where(diagonal, mask[...].astype(F32), 0.0).astype(BF16)
    out[0:side] = jnp.dot(spread, cotangent[...], preferred_element_type=F32).astype(BF16)
    rows = out.shape[0] - side
    index = lax.broadcasted_iota(jnp.int32, (rows, width), 0)
    block = jnp.zeros((rows, width), jnp.int32)
    for p in range(blocks):
        block = jnp.where(index == p, tile_rows[p] if blocks == slots else p, block)
    out[side:] = block.astype(F32).astype(BF16)


def stack_kernel(*refs):
    out, start = refs[-1], 0
    for block in refs[:-1]:
        out[start : start + block.shape[0]] = block[...]
        start += block.shape[0]


def forward_kernel(slots, n_col, blocks, ints, counts, tiles, *refs):
    n_row = len(refs) - 4
    sources, (out, count, held, total) = refs[:n_row], refs[n_row:]
    count[0] = jnp.max(counts[...])
    side = tiles.shape[-1]
    for q in range(n_row):
        held[q] = sources[q][...]
    me_row, live = lax.axis_index("row"), count[0]

    def product(s):
        taken = held[ints[slots + s] ^ me_row]
        value = jnp.dot(tiles[s], taken, preferred_element_type=F32)
        return jnp.where(s < live, value, 0.0)

    if blocks == slots:
        for s in range(slots):
            out[s * side : (s + 1) * side] = product(s).astype(BF16)
        return
    total[...] = jnp.zeros_like(total)

    def add(s):
        total[ints[s]] += product(s)

    each(slots, add)
    for t in range(n_col):
        out[t * side : (t + 1) * side] = total[t].astype(BF16)


def middle_kernel(slots, n_row, n_col, blocks, *refs):
    (ints, count), refs = refs[:2], refs[2:]
    (weight, bias, tiles, products), refs = refs[:4], refs[4:]
    steps = n_col.bit_length()
    cots, refs = refs[:steps], refs[steps:]
    hidden, sent, kept, kept_weight, total, agg, grads, grad_agg, weights, back, target = refs
    side = tiles.shape[-1]
    half = weight.shape[0] // 2
    me_row, me_col, live = lax.axis_index("row"), lax.axis_index("col"), count[0]
    each_rows = cots[0].shape[0]

    def cotangent(q, start, stop):
        step = q.bit_length()
        first = (q - (1 << step >> 1)) * each_rows
        return cots[step][first + start : first + stop]

    second = me_row % 2
    places_of = [
        me_col ^ jnp.where(second == 1, column_mask(1, q, n_col), column_mask(0, q, n_col))
        for q in range(n_col)
    ]
    for q in range(n_col):
        places = cotangent(q, side, each_rows)[:, 0:128].astype(F32).astype(jnp.int32)
        for p in range(blocks):
            target[places_of[q], p] = jnp.max(places[p : p + 1])
    total[...] = jnp.zeros_like(total)

    def add(i):
        c, p = i // blocks, i % blocks
        total[target[c, p]] += products[c, pl.ds(p * side, side), :].astype(F32)

    each(n_col * blocks, add)
    for q in range(n_col):
        t = places_of[q]
        rows = pl.ds(pl.multiple_of(t * side, side), side)
        aggregated = total[t].astype(BF16)
        agg[rows, :] = aggregated
        pre_act = jnp.dot(aggregated, weight[...], preferred_element_type=F32) + bias[...]
        sigma = jax.nn.sigmoid(pre_act)
        if q == 0:
            hidden[...] = (pre_act * sigma).astype(BF16)
        slope = sigma * (1.0 + pre_act * (1.0 - sigma))
        grad_pre = (cotangent(q, 0, side).astype(F32) * slope).astype(BF16)
        grads[rows, :] = grad_pre
        grad_agg[t] = lax.dot_general(
            grad_pre, weight[...], COLS_COLS, preferred_element_type=F32
        ).astype(BF16)
    back[...] = jnp.zeros_like(back)

    def put(s):
        value = lax.dot_general(
            tiles[s], grad_agg[ints[s]], ROWS_ROWS, preferred_element_type=F32
        )
        back[ints[slots + s] ^ me_row] += jnp.where(s < live, value, 0.0)

    each(slots, put)
    for m in range(n_row // 2):
        kept[m * side : (m + 1) * side] = back[2 * m]
        sent[m * side : (m + 1) * side] = back[2 * m + 1].astype(BF16)
    weights[...] = lax.dot_general(
        agg[...], grads[...], ROWS_ROWS, preferred_element_type=F32
    ).reshape(weights.shape)
    core = me_row % 2
    after = n_row // 2 * side
    kept_weight[...] = weights[core]
    sent[after : after + half] = weights[1 - core].astype(BF16)
    column_sum = jnp.sum(grads[...].astype(F32), axis=0, keepdims=True)
    sent[after + half : after + half + PAD] = two_halves(column_sum)


def chip_kernel(kept, kept_weight, own_sent, came, mine, *outs):
    half, side = kept_weight.shape[0], mine.shape[0]
    after = kept.shape[0]
    mine[...] = kept[0:side] + came[0:side].astype(F32)
    weights = (kept_weight[...] + came[after : after + half].astype(F32)).astype(BF16)
    ends = slice(after + half, after + half + PAD)
    column_sum = two_halves(joined(own_sent[ends]) + joined(came[ends]))
    n_line, second = len(outs) + 1, lax.axis_index("row") % 2
    for m, out in enumerate(outs, 1):
        chosen = jnp.where(second == 1, line_mask(1, m, n_line), line_mask(0, m, n_line))
        part = pl.ds(pl.multiple_of(chosen * side, side), side)
        out[0:side] = (kept[part, :] + came[part, :].astype(F32)).astype(BF16)
        out[side : side + half] = weights
        if carries_bias(m, n_line):
            out[side + half : side + half + PAD] = column_sum


def line_weight_kernel(scale, side, *refs):
    blocks, out = refs[:-1], refs[-1]
    n_line, half = len(blocks), out.shape[0] - 8
    start, ends = side + half, slice(side + half, side + half + PAD)
    out[0:half] = scale * tree_sum(b[side:start].astype(F32) for b in blocks)
    place = lax.broadcasted_iota(jnp.int32, (8, out.shape[1]), 0)
    rows = jnp.zeros((8, out.shape[1]), F32)
    for first in range(0, n_line, 4):
        heard = [joined(b[ends]) for m, b in enumerate(blocks) if first <= m < first + 4 and carries_bias(m, n_line)]
        rows = jnp.where(place == first // 2, scale * tree_sum(heard[:2]), rows)
        for block in heard[2:]:
            rows = jnp.where(place == first // 2 + 1, scale * block, rows)
    out[half:] = rows


def node_results_kernel(own_hidden, mine, *refs):
    blocks, (hidden, grad_features) = refs[:-2], refs[-2:]
    hidden[...] = own_hidden[...]
    side = mine.shape[0]
    total = mine[...]
    for block in blocks:
        total = total + block[0:side].astype(F32)
    grad_features[...] = total.astype(BF16)


def weight_results_kernel(n_line, own, other, grad_weight, grad_bias):
    half = grad_weight.shape[0] // 2
    for shift, block in enumerate((own, other)):
        start = pl.multiple_of((lax.axis_index("row") % 2 ^ shift) * half, half)
        grad_weight[pl.ds(start, half), :] = block[0:half]
    ours, theirs = own[half:], other[half:]
    grad_bias[...] = tree_sum(
        ours[i : i + 1] + (ours[i + 1 : i + 2] + theirs[i + 1 : i + 2]) for i in range(0, max(n_line // 2, 1), 2)
    )


def call(kernel, name, outs, scratch, ints, *arrays):
    need = sum(math.prod(shape) * jnp.dtype(dtype).itemsize for shape, dtype in scratch)

    def space(dtype):
        return pltpu.SMEM if dtype == jnp.int32 else pltpu.VMEM

    return pl.pallas_call(
        kernel,
        name=name,
        out_shape=[
            space(dtype)(shape, dtype) if stays else jax.ShapeDtypeStruct(shape, dtype)
            for shape, dtype, stays in outs
        ],
        in_specs=[pl.BlockSpec(memory_space=pltpu.SMEM)] * len(ints)
        + [pl.BlockSpec(memory_space=pltpu.VMEM)] * len(arrays),
        out_specs=[pl.BlockSpec(memory_space=space(dtype)) for _, dtype, _ in outs],
        scratch_shapes=[space(dtype)(shape, dtype) for shape, dtype in scratch],
        compiler_params=pltpu.CompilerParams(vmem_limit_bytes=need + 8 * 1024 * 1024),
    )(*ints, *arrays)


def near(array):
    return pltpu.with_memory_space_constraint(array, pltpu.VMEM)


def far(array):
    return pltpu.with_memory_space_constraint(array, pltpu.HBM)


def on_device(
    features, tiles, tile_rows, tile_cols, tile_count, weight, bias, cotangent, label_mask
):
    side = tiles.shape[-1]
    slots = tiles.shape[2]
    width = features.shape[2]
    n_row = lax.axis_size("row")
    n_col = lax.axis_size("col")
    n_line = n_row // 2
    blocks = min(slots, n_col)
    own_tiles = near(tiles[0, 0])

    own = features[0]
    along = [own] + [exchange(own, "row", 2 * m) for m in range(1, n_line)]

    with_places, own_bias, ints = call(
        functools.partial(cotangent_kernel, blocks),
        "masked_cotangent",
        [((side + blocks + -blocks % PAD, width), BF16, True), ((1, width), F32, True), ((2 * slots,), jnp.int32, True)],
        [],
        [far(tile_rows[0, 0]), far(tile_cols[0, 0])],
        far(label_mask),
        far(cotangent[0]),
        far(bias[None]),
    )
    ints = pltpu.with_memory_space_constraint(ints, pltpu.SMEM)
    cots, reach = [with_places], 1
    while reach < n_col:
        (held,) = call(
            stack_kernel,
            "cotangents_so_far",
            [((reach * with_places.shape[0], width), BF16, True)],
            [],
            [],
            *map(near, cots),
        ) if reach > 1 else cots
        cots, reach = cots + [column_exchange(held, reach)], 2 * reach

    sources = [own, exchange(own, "row", 1)]
    tile_count, _ = lax.optimization_barrier((tile_count, sources[1]))
    counts = jnp.broadcast_to(tile_count, (8, 128))
    for block in along[1:]:
        block, _ = lax.optimization_barrier((block, counts))
        sources += [block, exchange(block, "row", 1)]
    product, count = call(
        functools.partial(forward_kernel, slots, n_col, blocks),
        "tile_products",
        [((blocks * side, width), BF16, True), ((2,), jnp.int32, True)],
        [((n_row, side, width), BF16), ((n_col, side, width), F32)],
        [ints],
        near(counts),
        own_tiles,
        *map(near, sources),
    )
    products = lax.all_gather(product, "col")
    after = n_line * side
    half = width // 2
    hidden, sent, kept_back, kept_weight = call(
        functools.partial(middle_kernel, slots, n_row, n_col, blocks),
        "dense_layer",
        [
            ((side, width), BF16, True),
            ((after + half + PAD, width), BF16, True),
            ((after, width), F32, True),
            ((half, width), F32, True),
        ],
        [
            ((n_col, side, width), F32),
            ((n_col * side, width), BF16),
            ((n_col * side, width), BF16),
            ((n_col, side, width), BF16),
            ((2, half, width), F32),
            ((n_row, side, width), F32),
            ((n_col, blocks), jnp.int32),
        ],
        [ints, pltpu.with_memory_space_constraint(count, pltpu.SMEM)],
        near(weight),
        near(own_bias),
        own_tiles,
        near(products),
        *map(near, cots),
    )
    came = exchange(sent, "row", 1)
    mine, *parts = call(
        chip_kernel,
        "chip_sums",
        [((side, width), F32, True)]
        + [((side + half + PAD * carries_bias(m, n_line), width), BF16, True) for m in range(1, n_line)],
        [],
        [],
        *map(near, (kept_back, kept_weight, sent, came)),
    )
    line = [parts[0]] + [line_exchange(part, m) for m, part in enumerate(parts, 1)]
    scale = 1.0 / math.sqrt(n_row * n_col * side)
    (weights,) = call(
        functools.partial(line_weight_kernel, scale, side),
        "line_weight",
        [((half + 8, width), F32, True)],
        [],
        [],
        *map(near, line),
    )
    other_weights = exchange(weights, "row", 1)
    hidden, grad_features = call(
        node_results_kernel,
        "node_results",
        [((side, width), BF16, False), ((side, width), BF16, False)],
        [],
        [],
        *map(near, (hidden, mine, *line[1:])),
    )
    grad_weight, grad_bias = call(
        functools.partial(weight_results_kernel, n_line),
        "weight_results",
        [((width, width), F32, False), ((1, width), F32, False)],
        [],
        [],
        near(weights),
        near(other_weights),
    )
    return (hidden[None], grad_weight, grad_bias[0], grad_features[None])


def solution(mesh):
    return jax.shard_map(
        on_device,
        mesh=mesh,
        in_specs=(
            P("col", "row", None),
            P("row", "col", None, None, None),
            P("row", "col", None),
            P("row", "col", None),
            P("row", "col"),
            P(),
            P(),
            P("row", "col", None),
            P("row", "col"),
        ),
        out_specs=(P("row", "col", None), P(), P(), P("col", "row", None)),
        check_vma=False,
    )
```

```python
import functools
import math

import jax
import jax.numpy as jnp
from jax import lax
from jax.experimental import pallas as pl
from jax.experimental.pallas import tpu as pltpu
from jax.sharding import PartitionSpec as P

F32 = jnp.float32
BF16 = jnp.bfloat16
PAD = 16
ROWS_ROWS = (((0,), (0,)), ((), ()))
COLS_COLS = (((1,), (1,)), ((), ()))


def each(count, body):
    if count <= 16:
        for i in range(count):
            body(i)
    else:
        lax.fori_loop(0, count, lambda i, carry: (body(i), carry)[1], 0)


def exchange(value, axis, mask):
    size = lax.axis_size(axis)
    return lax.ppermute(value, axis, [(i, i ^ mask) for i in range(size)])


def column_mask(core, q, n_col):
    if n_col < 4 or core == 0:
        return q
    return q - q % 4 + (0, 2, 1, 3)[q % 4]


def column_exchange(value, q):
    rows, cols = lax.axis_size("row"), lax.axis_size("col")
    pairs = [(r * cols + c, r * cols + (c ^ column_mask(r % 2, q, cols))) for r in range(rows) for c in range(cols)]
    return lax.ppermute(value, ("row", "col"), pairs)


def line_mask(core, m, n_line):
    if n_line < 4 or core == 0:
        return m
    return m - m % 4 + (0, 1, 3, 2)[m % 4]


def carries_bias(m, n_line):
    return n_line < 4 or m % 4 != 3


def line_exchange(value, m):
    size = lax.axis_size("row")
    pairs = [(i, i ^ 2 * line_mask(i % 2, m, size // 2)) for i in range(size)]
    return lax.ppermute(value, "row", pairs)


def tree_sum(terms):
    terms = list(terms)
    while len(terms) > 1:
        terms = [a + b for a, b in zip(terms[::2], terms[1::2], strict=True)]
    return terms[0]


def two_halves(row):
    high = row.astype(BF16)
    low = (row - high.astype(F32)).astype(BF16)
    place = lax.broadcasted_iota(jnp.int32, (PAD, row.shape[-1]), 0)
    block = jnp.where(place == 0, high.astype(F32), jnp.where(place == 1, low.astype(F32), 0.0))
    return block.astype(BF16)


def joined(block):
    rows = block.astype(F32)
    return rows[0:1] + rows[1:2]


def cotangent_kernel(blocks, tile_rows, tile_cols, mask, cotangent, bias, out, own_bias, ints):
    own_bias[...] = bias[...]
    slots = tile_rows.shape[0]
    for s in range(slots):
        ints[s] = tile_rows[s]
        ints[slots + s] = tile_cols[s]
    side, width = cotangent.shape
    shape = (side, side)
    diagonal = lax.broadcasted_iota(jnp.int32, shape, 0) == lax.broadcasted_iota(jnp.int32, shape, 1)
    spread = jnp.where(diagonal, mask[...].astype(F32), 0.0).astype(BF16)
    out[0:side] = jnp.dot(spread, cotangent[...], preferred_element_type=F32).astype(BF16)
    rows = out.shape[0] - side
    index = lax.broadcasted_iota(jnp.int32, (rows, width), 0)
    block = jnp.zeros((rows, width), jnp.int32)
    for p in range(blocks):
        block = jnp.where(index == p, tile_rows[p] if blocks == slots else p, block)
    out[side:] = block.astype(F32).astype(BF16)


def stack_kernel(*refs):
    out, start = refs[-1], 0
    for block in refs[:-1]:
        out[start : start + block.shape[0]] = block[...]
        start += block.shape[0]


def forward_kernel(slots, n_col, blocks, ints, counts, tiles, *refs):
    n_row = len(refs) - 4
    sources, (out, count, held, total) = refs[:n_row], refs[n_row:]
    count[0] = jnp.max(counts[...])
    side = tiles.shape[-1]
    for q in range(n_row):
        held[q] = sources[q][...]
    me_row, live = lax.axis_index("row"), count[0]

    def product(s):
        taken = held[ints[slots + s] ^ me_row]
        value = jnp.dot(tiles[s], taken, preferred_element_type=F32)
        return jnp.where(s < live, value, 0.0)

    if blocks == slots:
        for s in range(slots):
            out[s * side : (s + 1) * side] = product(s).astype(BF16)
        return
    total[...] = jnp.zeros_like(total)

    def add(s):
        total[ints[s]] += product(s)

    each(slots, add)
    for t in range(n_col):
        out[t * side : (t + 1) * side] = total[t].astype(BF16)


def middle_kernel(slots, n_row, n_col, blocks, *refs):
    (ints, count), refs = refs[:2], refs[2:]
    (weight, bias, tiles, products), refs = refs[:4], refs[4:]
    steps = n_col.bit_length()
    cots, refs = refs[:steps], refs[steps:]
    hidden, sent, kept, kept_weight, total, agg, grads, grad_agg, weights, back, target = refs
    side = tiles.shape[-1]
    half = weight.shape[0] // 2
    me_row, me_col, live = lax.axis_index("row"), lax.axis_index("col"), count[0]
    each_rows = cots[0].shape[0]

    def cotangent(q, start, stop):
        step = q.bit_length()
        first = (q - (1 << step >> 1)) * each_rows
        return cots[step][first + start : first + stop]

    second = me_row % 2
    places_of = [
        me_col ^ jnp.where(second == 1, column_mask(1, q, n_col), column_mask(0, q, n_col))
        for q in range(n_col)
    ]
    for q in range(n_col):
        places = jnp.max(cotangent(q, side, each_rows)[:, 0:128].astype(F32), axis=1, keepdims=True)
        for p in range(blocks):
            target[places_of[q], p] = places[p, 0].astype(jnp.int32)
    total[...] = jnp.zeros_like(total)

    def add(i):
        c, p = i // blocks, i % blocks
        total[target[c, p]] += products[c, pl.ds(p * side, side), :].astype(F32)

    each(n_col * blocks, add)
    for q in range(n_col):
        t = places_of[q]
        rows = pl.ds(pl.multiple_of(t * side, side), side)
        aggregated = total[t].astype(BF16)
        agg[rows, :] = aggregated
        pre_act = jnp.dot(aggregated, weight[...], preferred_element_type=F32) + bias[...]
        sigma = jax.nn.sigmoid(pre_act)
        if q == 0:
            hidden[...] = (pre_act * sigma).astype(BF16)
        slope = sigma * (1.0 + pre_act * (1.0 - sigma))
        grad_pre = (cotangent(q, 0, side).astype(F32) * slope).astype(BF16)
        grads[rows, :] = grad_pre
        grad_agg[t] = lax.dot_general(
            grad_pre, weight[...], COLS_COLS, preferred_element_type=F32
        ).astype(BF16)
    back[...] = jnp.zeros_like(back)

    def put(s):
        value = lax.dot_general(
            tiles[s], grad_agg[ints[s]], ROWS_ROWS, preferred_element_type=F32
        )
        back[ints[slots + s] ^ me_row] += jnp.where(s < live, value, 0.0)

    each(slots, put)
    for m in range(n_row // 2):
        kept[m * side : (m + 1) * side] = back[2 * m]
        sent[m * side : (m + 1) * side] = back[2 * m + 1].astype(BF16)
    weights[...] = lax.dot_general(
        agg[...], grads[...], ROWS_ROWS, preferred_element_type=F32
    ).reshape(weights.shape)
    core = me_row % 2
    after = n_row // 2 * side
    kept_weight[...] = weights[core]
    sent[after : after + half] = weights[1 - core].astype(BF16)
    column_sum = jnp.sum(grads[...].astype(F32), axis=0, keepdims=True)
    sent[after + half : after + half + PAD] = two_halves(column_sum)


def chip_kernel(kept, kept_weight, own_sent, came, mine, *outs):
    half, side = kept_weight.shape[0], mine.shape[0]
    after = kept.shape[0]
    mine[...] = kept[0:side] + came[0:side].astype(F32)
    weights = (kept_weight[...] + came[after : after + half].astype(F32)).astype(BF16)
    ends = slice(after + half, after + half + PAD)
    column_sum = two_halves(joined(own_sent[ends]) + joined(came[ends]))
    n_line, second = len(outs) + 1, lax.axis_index("row") % 2
    for m, out in enumerate(outs, 1):
        chosen = jnp.where(second == 1, line_mask(1, m, n_line), line_mask(0, m, n_line))
        part = pl.ds(pl.multiple_of(chosen * side, side), side)
        out[0:side] = (kept[part, :] + came[part, :].astype(F32)).astype(BF16)
        out[side : side + half] = weights
        if carries_bias(m, n_line):
            out[side + half : side + half + PAD] = column_sum


def line_weight_kernel(scale, side, *refs):
    blocks, out = refs[:-1], refs[-1]
    n_line, half = len(blocks), out.shape[0] - 8
    start, ends = side + half, slice(side + half, side + half + PAD)
    out[0:half] = scale * tree_sum(b[side:start].astype(F32) for b in blocks)
    place = lax.broadcasted_iota(jnp.int32, (8, out.shape[1]), 0)
    rows = jnp.zeros((8, out.shape[1]), F32)
    for first in range(0, n_line, 4):
        heard = [joined(b[ends]) for m, b in enumerate(blocks) if first <= m < first + 4 and carries_bias(m, n_line)]
        rows = jnp.where(place == first // 2, scale * tree_sum(heard[:2]), rows)
        for block in heard[2:]:
            rows = jnp.where(place == first // 2 + 1, scale * block, rows)
    out[half:] = rows


def node_results_kernel(own_hidden, mine, *refs):
    blocks, (hidden, grad_features) = refs[:-2], refs[-2:]
    hidden[...] = own_hidden[...]
    side = mine.shape[0]
    total = mine[...]
    for block in blocks:
        total = total + block[0:side].astype(F32)
    grad_features[...] = total.astype(BF16)


def weight_results_kernel(n_line, own, other, grad_weight, grad_bias):
    half = grad_weight.shape[0] // 2
    for shift, block in enumerate((own, other)):
        start = pl.multiple_of((lax.axis_index("row") % 2 ^ shift) * half, half)
        grad_weight[pl.ds(start, half), :] = block[0:half]
    ours, theirs = own[half:], other[half:]
    grad_bias[...] = tree_sum(
        ours[i : i + 1] + (ours[i + 1 : i + 2] + theirs[i + 1 : i + 2]) for i in range(0, max(n_line // 2, 1), 2)
    )


def call(kernel, name, outs, scratch, ints, *arrays):
    need = sum(math.prod(shape) * jnp.dtype(dtype).itemsize for shape, dtype in scratch)

    def space(dtype):
        return pltpu.SMEM if dtype == jnp.int32 else pltpu.VMEM

    return pl.pallas_call(
        kernel,
        name=name,
        out_shape=[
            space(dtype)(shape, dtype) if stays else jax.ShapeDtypeStruct(shape, dtype)
            for shape, dtype, stays in outs
        ],
        in_specs=[pl.BlockSpec(memory_space=pltpu.SMEM)] * len(ints)
        + [pl.BlockSpec(memory_space=pltpu.VMEM)] * len(arrays),
        out_specs=[pl.BlockSpec(memory_space=space(dtype)) for _, dtype, _ in outs],
        scratch_shapes=[space(dtype)(shape, dtype) for shape, dtype in scratch],
        compiler_params=pltpu.CompilerParams(vmem_limit_bytes=need + 8 * 1024 * 1024),
    )(*ints, *arrays)


def near(array):
    return pltpu.with_memory_space_constraint(array, pltpu.VMEM)


def far(array):
    return pltpu.with_memory_space_constraint(array, pltpu.HBM)


def on_device(
    features, tiles, tile_rows, tile_cols, tile_count, weight, bias, cotangent, label_mask
):
    side = tiles.shape[-1]
    slots = tiles.shape[2]
    width = features.shape[2]
    n_row = lax.axis_size("row")
    n_col = lax.axis_size("col")
    n_line = n_row // 2
    blocks = min(slots, n_col)
    own_tiles = near(tiles[0, 0])

    own = features[0]
    along = [own] + [exchange(own, "row", 2 * m) for m in range(1, n_line)]

    with_places, own_bias, ints = call(
        functools.partial(cotangent_kernel, blocks),
        "masked_cotangent",
        [((side + blocks + -blocks % PAD, width), BF16, True), ((1, width), F32, True), ((2 * slots,), jnp.int32, True)],
        [],
        [far(tile_rows[0, 0]), far(tile_cols[0, 0])],
        far(label_mask),
        far(cotangent[0]),
        far(bias[None]),
    )
    ints = pltpu.with_memory_space_constraint(ints, pltpu.SMEM)
    cots, reach = [with_places], 1
    while reach < n_col:
        (held,) = call(
            stack_kernel,
            "cotangents_so_far",
            [((reach * with_places.shape[0], width), BF16, True)],
            [],
            [],
            *map(near, cots),
        ) if reach > 1 else cots
        cots, reach = cots + [column_exchange(held, reach)], 2 * reach

    sources = [own, exchange(own, "row", 1)]
    tile_count, _ = lax.optimization_barrier((tile_count, sources[1]))
    counts = jnp.broadcast_to(tile_count, (8, 128))
    for block in along[1:]:
        block, _ = lax.optimization_barrier((block, counts))
        sources += [block, exchange(block, "row", 1)]
    product, count = call(
        functools.partial(forward_kernel, slots, n_col, blocks),
        "tile_products",
        [((blocks * side, width), BF16, True), ((2,), jnp.int32, True)],
        [((n_row, side, width), BF16), ((n_col, side, width), F32)],
        [ints],
        near(counts),
        own_tiles,
        *map(near, sources),
    )
    products = lax.all_gather(product, "col")
    after = n_line * side
    half = width // 2
    hidden, sent, kept_back, kept_weight = call(
        functools.partial(middle_kernel, slots, n_row, n_col, blocks),
        "dense_layer",
        [
            ((side, width), BF16, True),
            ((after + half + PAD, width), BF16, True),
            ((after, width), F32, True),
            ((half, width), F32, True),
        ],
        [
            ((n_col, side, width), F32),
            ((n_col * side, width), BF16),
            ((n_col * side, width), BF16),
            ((n_col, side, width), BF16),
            ((2, half, width), F32),
            ((n_row, side, width), F32),
            ((n_col, blocks), jnp.int32),
        ],
        [ints, pltpu.with_memory_space_constraint(count, pltpu.SMEM)],
        near(weight),
        near(own_bias),
        own_tiles,
        near(products),
        *map(near, cots),
    )
    came = exchange(sent, "row", 1)
    mine, *parts = call(
        chip_kernel,
        "chip_sums",
        [((side, width), F32, True)]
        + [((side + half + PAD * carries_bias(m, n_line), width), BF16, True) for m in range(1, n_line)],
        [],
        [],
        *map(near, (kept_back, kept_weight, sent, came)),
    )
    line = [parts[0]] + [line_exchange(part, m) for m, part in enumerate(parts, 1)]
    scale = 1.0 / math.sqrt(n_row * n_col * side)
    (weights,) = call(
        functools.partial(line_weight_kernel, scale, side),
        "line_weight",
        [((half + 8, width), F32, True)],
        [],
        [],
        *map(near, line),
    )
    other_weights = exchange(weights, "row", 1)
    hidden, grad_features = call(
        node_results_kernel,
        "node_results",
        [((side, width), BF16, False), ((side, width), BF16, False)],
        [],
        [],
        *map(near, (hidden, mine, *line[1:])),
    )
    grad_weight, grad_bias = call(
        functools.partial(weight_results_kernel, n_line),
        "weight_results",
        [((width, width), F32, False), ((1, width), F32, False)],
        [],
        [],
        near(weights),
        near(other_weights),
    )
    return (hidden[None], grad_weight, grad_bias[0], grad_features[None])


def solution(mesh):
    return jax.shard_map(
        on_device,
        mesh=mesh,
        in_specs=(
            P("col", "row", None),
            P("row", "col", None, None, None),
            P("row", "col", None),
            P("row", "col", None),
            P("row", "col"),
            P(),
            P(),
            P("row", "col", None),
            P("row", "col"),
        ),
        out_specs=(P("row", "col", None), P(), P(), P("col", "row", None)),
        check_vma=False,
    )
```

```python
import functools
import math

import jax
import jax.numpy as jnp
from jax import lax
from jax.experimental import pallas as pl
from jax.experimental.pallas import tpu as pltpu
from jax.sharding import PartitionSpec as P

F32 = jnp.float32
BF16 = jnp.bfloat16
PAD = 16
ROWS_ROWS = (((0,), (0,)), ((), ()))
COLS_COLS = (((1,), (1,)), ((), ()))


def each(count, body):
    if count <= 16:
        for i in range(count):
            body(i)
    else:
        lax.fori_loop(0, count, lambda i, carry: (body(i), carry)[1], 0)


def exchange(value, axis, mask):
    size = lax.axis_size(axis)
    return lax.ppermute(value, axis, [(i, i ^ mask) for i in range(size)])


def column_mask(core, q, n_col):
    if n_col < 4 or core == 0:
        return q
    return q - q % 4 + (0, 2, 1, 3)[q % 4]


def column_exchange(value, q):
    rows, cols = lax.axis_size("row"), lax.axis_size("col")
    pairs = [(r * cols + c, r * cols + (c ^ column_mask(r % 2, q, cols))) for r in range(rows) for c in range(cols)]
    return lax.ppermute(value, ("row", "col"), pairs)


def line_mask(core, m, n_line):
    if n_line < 4 or core == 0:
        return m
    return m - m % 4 + (0, 1, 3, 2)[m % 4]


def carries_bias(m, n_line):
    return n_line < 4 or m % 4 != 3


def line_exchange(value, m):
    size = lax.axis_size("row")
    pairs = [(i, i ^ 2 * line_mask(i % 2, m, size // 2)) for i in range(size)]
    return lax.ppermute(value, "row", pairs)


def tree_sum(terms):
    terms = list(terms)
    while len(terms) > 1:
        terms = [a + b for a, b in zip(terms[::2], terms[1::2], strict=True)]
    return terms[0]


def two_halves(row):
    high = row.astype(BF16)
    low = (row - high.astype(F32)).astype(BF16)
    place = lax.broadcasted_iota(jnp.int32, (PAD, row.shape[-1]), 0)
    block = jnp.where(place == 0, high.astype(F32), jnp.where(place == 1, low.astype(F32), 0.0))
    return block.astype(BF16)


def joined(block):
    rows = block.astype(F32)
    return rows[0:1] + rows[1:2]


def cotangent_kernel(blocks, tile_rows, tile_cols, mask, cotangent, bias, out, own_bias, ints):
    own_bias[...] = bias[...]
    slots = tile_rows.shape[0]
    for s in range(slots):
        ints[s] = tile_rows[s]
        ints[slots + s] = tile_cols[s]
    side, width = cotangent.shape
    shape = (side, side)
    diagonal = lax.broadcasted_iota(jnp.int32, shape, 0) == lax.broadcasted_iota(jnp.int32, shape, 1)
    spread = jnp.where(diagonal, mask[...].astype(F32), 0.0).astype(BF16)
    out[0:side] = jnp.dot(spread, cotangent[...], preferred_element_type=F32).astype(BF16)
    rows = out.shape[0] - side
    index = lax.broadcasted_iota(jnp.int32, (rows, width), 0)
    block = jnp.zeros((rows, width), jnp.int32)
    for p in range(blocks):
        block = jnp.where(index == p, tile_rows[p] if blocks == slots else p, block)
    out[side:] = block.astype(F32).astype(BF16)


def stack_kernel(*refs):
    out, start = refs[-1], 0
    for block in refs[:-1]:
        out[start : start + block.shape[0]] = block[...]
        start += block.shape[0]


def forward_kernel(slots, n_col, blocks, ints, counts, tiles, *refs):
    n_row = len(refs) - 4
    sources, (out, count, held, total) = refs[:n_row], refs[n_row:]
    count[0] = jnp.max(counts[...])
    side = tiles.shape[-1]
    for q in range(n_row):
        held[q] = sources[q][...]
    me_row, live = lax.axis_index("row"), count[0]

    def product(s):
        taken = held[ints[slots + s] ^ me_row]
        value = jnp.dot(tiles[s], taken, preferred_element_type=F32)
        return jnp.where(s < live, value, 0.0)

    if blocks == slots:
        for s in range(slots):
            out[s * side : (s + 1) * side] = product(s).astype(BF16)
        return
    total[...] = jnp.zeros_like(total)

    def add(s):
        total[ints[s]] += product(s)

    each(slots, add)
    for t in range(n_col):
        out[t * side : (t + 1) * side] = total[t].astype(BF16)


def middle_kernel(slots, n_row, n_col, blocks, *refs):
    (ints, count), refs = refs[:2], refs[2:]
    (weight, bias, tiles, products), refs = refs[:4], refs[4:]
    steps = n_col.bit_length()
    cots, refs = refs[:steps], refs[steps:]
    hidden, sent, kept, kept_weight, total, agg, grads, grad_agg, weights, back, target = refs
    side = tiles.shape[-1]
    half = weight.shape[0] // 2
    me_row, me_col, live = lax.axis_index("row"), lax.axis_index("col"), count[0]
    each_rows = cots[0].shape[0]

    def cotangent(q, start, stop):
        step = q.bit_length()
        first = (q - (1 << step >> 1)) * each_rows
        return cots[step][first + start : first + stop]

    second = me_row % 2
    places_of = [
        me_col ^ jnp.where(second == 1, column_mask(1, q, n_col), column_mask(0, q, n_col))
        for q in range(n_col)
    ]
    for q in range(n_col):
        places = jnp.max(cotangent(q, side, each_rows)[:, 0:128].astype(F32), axis=1, keepdims=True)
        for p in range(blocks):
            target[places_of[q], p] = places[p, 0].astype(jnp.int32)
    total[...] = jnp.zeros_like(total)

    def add(i):
        c, p = i // blocks, i % blocks
        total[target[c, p]] += products[c, pl.ds(p * side, side), :].astype(F32)

    each(n_col * blocks, add)
    for q in range(n_col):
        t = places_of[q]
        rows = pl.ds(pl.multiple_of(t * side, side), side)
        aggregated = total[t].astype(BF16)
        agg[rows, :] = aggregated
        pre_act = jnp.dot(aggregated, weight[...], preferred_element_type=F32) + bias[...]
        sigma = jax.nn.sigmoid(pre_act)
        if q == 0:
            hidden[...] = (pre_act * sigma).astype(BF16)
        slope = sigma * (1.0 + pre_act * (1.0 - sigma))
        grad_pre = (cotangent(q, 0, side).astype(F32) * slope).astype(BF16)
        grads[rows, :] = grad_pre
        grad_agg[t] = lax.dot_general(
            grad_pre, weight[...], COLS_COLS, preferred_element_type=F32
        ).astype(BF16)
    back[...] = jnp.zeros_like(back)

    def put(s):
        value = lax.dot_general(
            tiles[s], grad_agg[ints[s]], ROWS_ROWS, preferred_element_type=F32
        )
        back[ints[slots + s] ^ me_row] += jnp.where(s < live, value, 0.0)

    each(slots, put)
    for m in range(n_row // 2):
        kept[m * side : (m + 1) * side] = back[2 * m]
        sent[m * side : (m + 1) * side] = back[2 * m + 1].astype(BF16)
    weights[...] = lax.dot_general(
        agg[...], grads[...], ROWS_ROWS, preferred_element_type=F32
    ).reshape(weights.shape)
    core = me_row % 2
    after = n_row // 2 * side
    kept_weight[...] = weights[core]
    sent[after : after + half] = weights[1 - core].astype(BF16)
    column_sum = jnp.sum(grads[...].astype(F32), axis=0, keepdims=True)
    sent[after + half : after + half + PAD] = two_halves(column_sum)


def chip_kernel(kept, kept_weight, own_sent, came, mine, *outs):
    half, side = kept_weight.shape[0], mine.shape[0]
    after = kept.shape[0]
    mine[...] = kept[0:side] + came[0:side].astype(F32)
    weights = (kept_weight[...] + came[after : after + half].astype(F32)).astype(BF16)
    ends = slice(after + half, after + half + PAD)
    column_sum = two_halves(joined(own_sent[ends]) + joined(came[ends]))
    n_line, second = len(outs) + 1, lax.axis_index("row") % 2
    for m, out in enumerate(outs, 1):
        chosen = jnp.where(second == 1, line_mask(1, m, n_line), line_mask(0, m, n_line))
        part = pl.ds(pl.multiple_of(chosen * side, side), side)
        out[0:side] = (kept[part, :] + came[part, :].astype(F32)).astype(BF16)
        out[side : side + half] = weights
        if carries_bias(m, n_line):
            out[side + half : side + half + PAD] = column_sum


def line_weight_kernel(scale, side, *refs):
    blocks, out = refs[:-1], refs[-1]
    n_line, half = len(blocks), out.shape[0] - 8
    start, ends = side + half, slice(side + half, side + half + PAD)
    out[0:half] = scale * tree_sum(b[side:start].astype(F32) for b in blocks)
    place = lax.broadcasted_iota(jnp.int32, (8, out.shape[1]), 0)
    rows = jnp.zeros((8, out.shape[1]), F32)
    for first in range(0, n_line, 4):
        heard = [joined(b[ends]) for m, b in enumerate(blocks) if first <= m < first + 4 and carries_bias(m, n_line)]
        rows = jnp.where(place == first // 2, scale * tree_sum(heard[:2]), rows)
        for block in heard[2:]:
            rows = jnp.where(place == first // 2 + 1, scale * block, rows)
    out[half:] = rows


def node_results_kernel(own_hidden, mine, *refs):
    blocks, (hidden, grad_features) = refs[:-2], refs[-2:]
    hidden[...] = own_hidden[...]
    side = mine.shape[0]
    total = mine[...]
    for block in blocks:
        total = total + block[0:side].astype(F32)
    grad_features[...] = total.astype(BF16)


def weight_results_kernel(n_line, own, other, grad_weight, grad_bias):
    half = grad_weight.shape[0] // 2
    for shift, block in enumerate((own, other)):
        start = pl.multiple_of((lax.axis_index("row") % 2 ^ shift) * half, half)
        grad_weight[pl.ds(start, half), :] = block[0:half]
    ours, theirs = own[half:], other[half:]
    grad_bias[...] = tree_sum(
        ours[i : i + 1] + (ours[i + 1 : i + 2] + theirs[i + 1 : i + 2]) for i in range(0, max(n_line // 2, 1), 2)
    )


def call(kernel, name, outs, scratch, ints, *arrays):
    need = sum(math.prod(shape) * jnp.dtype(dtype).itemsize for shape, dtype in scratch)

    def space(dtype):
        return pltpu.SMEM if dtype == jnp.int32 else pltpu.VMEM

    return pl.pallas_call(
        kernel,
        name=name,
        out_shape=[
            space(dtype)(shape, dtype) if stays else jax.ShapeDtypeStruct(shape, dtype)
            for shape, dtype, stays in outs
        ],
        in_specs=[pl.BlockSpec(memory_space=pltpu.SMEM)] * len(ints)
        + [pl.BlockSpec(memory_space=pltpu.VMEM)] * len(arrays),
        out_specs=[pl.BlockSpec(memory_space=space(dtype)) for _, dtype, _ in outs],
        scratch_shapes=[space(dtype)(shape, dtype) for shape, dtype in scratch],
        cost_estimate=pl.CostEstimate(flops=0, bytes_accessed=0, transcendentals=0),
        compiler_params=pltpu.CompilerParams(vmem_limit_bytes=need + 8 * 1024 * 1024),
    )(*ints, *arrays)


def near(array):
    return pltpu.with_memory_space_constraint(array, pltpu.VMEM)


def far(array):
    return pltpu.with_memory_space_constraint(array, pltpu.HBM)


def on_device(
    features, tiles, tile_rows, tile_cols, tile_count, weight, bias, cotangent, label_mask
):
    side = tiles.shape[-1]
    slots = tiles.shape[2]
    width = features.shape[2]
    n_row = lax.axis_size("row")
    n_col = lax.axis_size("col")
    n_line = n_row // 2
    blocks = min(slots, n_col)
    own_tiles = near(tiles[0, 0])

    own = features[0]
    along = [own] + [exchange(own, "row", 2 * m) for m in range(1, n_line)]

    with_places, own_bias, ints = call(
        functools.partial(cotangent_kernel, blocks),
        "masked_cotangent",
        [((side + blocks + -blocks % PAD, width), BF16, True), ((1, width), F32, True), ((2 * slots,), jnp.int32, True)],
        [],
        [far(tile_rows[0, 0]), far(tile_cols[0, 0])],
        far(label_mask),
        far(cotangent[0]),
        far(bias[None]),
    )
    ints = pltpu.with_memory_space_constraint(ints, pltpu.SMEM)
    cots, reach = [with_places], 1
    while reach < n_col:
        (held,) = call(
            stack_kernel,
            "cotangents_so_far",
            [((reach * with_places.shape[0], width), BF16, True)],
            [],
            [],
            *map(near, cots),
        ) if reach > 1 else cots
        cots, reach = cots + [column_exchange(held, reach)], 2 * reach

    sources = [own, exchange(own, "row", 1)]
    tile_count, _ = lax.optimization_barrier((tile_count, sources[1]))
    counts = jnp.broadcast_to(tile_count, (8, 128))
    for block in along[1:]:
        block, _ = lax.optimization_barrier((block, counts))
        sources += [block, exchange(block, "row", 1)]
    product, count = call(
        functools.partial(forward_kernel, slots, n_col, blocks),
        "tile_products",
        [((blocks * side, width), BF16, True), ((2,), jnp.int32, True)],
        [((n_row, side, width), BF16), ((n_col, side, width), F32)],
        [ints],
        near(counts),
        own_tiles,
        *map(near, sources),
    )
    products = lax.all_gather(product, "col")
    after = n_line * side
    half = width // 2
    hidden, sent, kept_back, kept_weight = call(
        functools.partial(middle_kernel, slots, n_row, n_col, blocks),
        "dense_layer",
        [
            ((side, width), BF16, True),
            ((after + half + PAD, width), BF16, True),
            ((after, width), F32, True),
            ((half, width), F32, True),
        ],
        [
            ((n_col, side, width), F32),
            ((n_col * side, width), BF16),
            ((n_col * side, width), BF16),
            ((n_col, side, width), BF16),
            ((2, half, width), F32),
            ((n_row, side, width), F32),
            ((n_col, blocks), jnp.int32),
        ],
        [ints, pltpu.with_memory_space_constraint(count, pltpu.SMEM)],
        near(weight),
        near(own_bias),
        own_tiles,
        near(products),
        *map(near, cots),
    )
    came = exchange(sent, "row", 1)
    mine, *parts = call(
        chip_kernel,
        "chip_sums",
        [((side, width), F32, True)]
        + [((side + half + PAD * carries_bias(m, n_line), width), BF16, True) for m in range(1, n_line)],
        [],
        [],
        *map(near, (kept_back, kept_weight, sent, came)),
    )
    line = [parts[0]] + [line_exchange(part, m) for m, part in enumerate(parts, 1)]
    scale = 1.0 / math.sqrt(n_row * n_col * side)
    (weights,) = call(
        functools.partial(line_weight_kernel, scale, side),
        "line_weight",
        [((half + 8, width), F32, True)],
        [],
        [],
        *map(near, line),
    )
    other_weights = exchange(weights, "row", 1)
    hidden, grad_features = call(
        node_results_kernel,
        "node_results",
        [((side, width), BF16, False), ((side, width), BF16, False)],
        [],
        [],
        *map(near, (hidden, mine, *line[1:])),
    )
    grad_weight, grad_bias = call(
        functools.partial(weight_results_kernel, n_line),
        "weight_results",
        [((width, width), F32, False), ((1, width), F32, False)],
        [],
        [],
        near(weights),
        near(other_weights),
    )
    return (hidden[None], grad_weight, grad_bias[0], grad_features[None])


def solution(mesh):
    return jax.shard_map(
        on_device,
        mesh=mesh,
        in_specs=(
            P("col", "row", None),
            P("row", "col", None, None, None),
            P("row", "col", None),
            P("row", "col", None),
            P("row", "col"),
            P(),
            P(),
            P("row", "col", None),
            P("row", "col"),
        ),
        out_specs=(P("row", "col", None), P(), P(), P("col", "row", None)),
        check_vma=False,
    )
```
